128 devices in a mesh: dom: 32 (over y, z_hi, x), orb: 4 (over z_lo, core).
Axes of the slice: x: 4, y: 4, z: 4 (z_hi: 2, z_lo: 2; z = z_hi * 2 + z_lo), core: 2. Of those that a mesh axis runs over, the one named last changes fastest.
Arguments:
- orbitals: float32 [32, 384, 2048], P('orb', 'dom'), may hold values from -40 to 40, as said below
- potential: float32 [384, 2048], P('dom'), may hold values from -2 to 1
- subspace: bfloat16 [2048, 384, 2048], P('orb', 'dom'), may hold values from -0.0068359375 to 0.0068359375
Outputs:
- correlation: float32 [32, 2048], P('dom', 'orb')
- projected: float32 [32, 2048], P('dom', 'orb')
The draws below stay inside these ranges and needn't reach their ends.
Inputs may be any that keep to these rules, and one draw needn't show every extreme that they name: orbitals of the block, real-valued.
All inputs are finite; a program needn't handle non-finite values.
Results may differ from the reference program's by a relative error of at most 0.0021.
The reference program's roundings to bfloat16 on the way (of `filtered` and `applied`) count: a program that leaves them out, or rounds other values in their place, can miss the bound.
Values may be sent and summed in bfloat16 or wider, within the bound.
A program may use at most 192 MiB of HBM per device.

```python
import jax
import jax.numpy as jnp
from jax import lax

BLOCK = 32
NORB = 2048
NZ = 64
PLANE = 2048
NX = 384
CELLS = 786432


def draw_orbitals(key, part):
    key = jax.random.fold_in(key, 7)
    first_key = jax.random.fold_in(key, 0)
    position = jnp.arange(NX, dtype=jnp.float32) / NX
    envelope = (1.0 + position)[None, :, None]
    base = jnp.clip(jax.random.normal(first_key, (BLOCK, NX, PLANE), jnp.float32), -4.0, 4.0)
    return base * envelope


def steps_of(own_key, shape, pieces, least, top_value):
    def one(dim, blocks):
        heights = jax.random.uniform(jax.random.fold_in(jax.random.fold_in(own_key, 6), dim), (blocks,), jnp.float32, least / len(pieces), top_value / len(pieces))
        return jnp.repeat(jnp.exp(heights), shape[dim] // blocks).reshape((-1,) + (1,) * (len(shape) - dim - 1))

    loudness = one(*pieces[0])
    for cut in pieces[1:]:
        loudness = loudness * one(*cut)
    return loudness


def scatter_about(key, extent, scale, reach, cuts=(), kind=jnp.bfloat16):
    entries = jax.random.normal(key, extent, jnp.float32) * scale
    if len(cuts) > 0:
        entries = steps_of(key, extent, cuts, -0.22, 0.18) * entries
    return jnp.clip(entries, min=-reach, max=reach).astype(kind)


def setup_inputs(seed: int = 0) -> dict:
    seeds = jax.random.split(jax.random.key(seed), 4)
    return {
        "orbitals": draw_orbitals(jax.random.fold_in(seeds[3], 71), 0),
        "potential": jnp.clip(-2.0 + 3.0 * jax.random.uniform(seeds[1], (NX, PLANE), jnp.float32) ** steps_of(seeds[1], (NX, PLANE), ((0, 32),), -0.2, 0.2), -2.0, 1.0),
        "subspace": scatter_about(seeds[2], (NORB, NX, PLANE), CELLS ** -0.5, 0.0068359375, ((0, 4), (1, 32))),
    }


coeffs = (-5369.0 / 1800.0, 12.0 / 7.0, -15.0 / 56.0, 10.0 / 189.0, -1.0 / 112.0, 2.0 / 1925.0, -1.0 / 16632.0)

def hamiltonian(padded, potential):
    length = padded.shape[1] - 12
    center = padded[:, 6:6 + length]
    depth = center.shape[2]
    zpos = (jnp.arange(depth, dtype=jnp.int32) % NZ)[None, None, :]
    total = 3.0 * coeffs[0] * center
    for shift_k in range(1, 7):
        along = padded[:, 6 + shift_k:6 + shift_k + length] + padded[:, 6 - shift_k:6 - shift_k + length]
        along = along + jnp.roll(center, shift_k * NZ, 2) + jnp.roll(center, -shift_k * NZ, 2)
        lower = jnp.where(zpos >= shift_k, jnp.roll(center, shift_k, 2), jnp.roll(center, shift_k - NZ, 2))
        upper = jnp.where(zpos < NZ - shift_k, jnp.roll(center, -shift_k, 2), jnp.roll(center, NZ - shift_k, 2))
        along = along + lower + upper
        total = total + coeffs[shift_k] * along
    return -0.5 * total + potential[None] * center

def periodic(field):
    return jnp.concatenate([field[:, -6:], field, field[:, :6]], axis=1)

def reference(orbitals, potential, subspace):
    first = (hamiltonian(periodic(orbitals), potential) - 8.0 * orbitals) / 8.0
    second = 2.0 * (hamiltonian(periodic(first), potential) - 8.0 * first) / 8.0 - orbitals
    filtered = second.astype(jnp.bfloat16).reshape(BLOCK, CELLS)
    applied = hamiltonian(periodic(second), potential).astype(jnp.bfloat16).reshape(BLOCK, CELLS)
    squares = lax.optimization_barrier(jnp.sum(jnp.square(filtered.astype(jnp.float32)), axis=1))
    scale = jnp.sqrt(squares / CELLS + 1e-06)
    stacked = jnp.concatenate([filtered, applied], axis=0)
    flat_sub = subspace.reshape(NORB, CELLS)
    gram = jnp.dot(stacked, flat_sub.T, preferred_element_type=jnp.float32)
    correlation = gram[:BLOCK] / scale[:, None]
    projected = gram[BLOCK:] / scale[:, None]
    return (correlation, projected)
```

```python
import jax
import jax.numpy as jnp
from jax import lax
from jax.experimental import pallas as pl
from jax.experimental.pallas import tpu as pltpu
from jax.sharding import PartitionSpec as P

BF = jnp.bfloat16
F32 = jnp.float32
MESH = pl.DeviceIdType.MESH

coeffs = (
    -5369.0 / 1800.0,
    12.0 / 7.0,
    -15.0 / 56.0,
    10.0 / 189.0,
    -1.0 / 112.0,
    2.0 / 1925.0,
    -1.0 / 16632.0,
)
A = [-0.5 * c for c in coeffs]

NZ = 64
PLANE = 2048
EXT = 384
GROUP = 4
DOM = 32
CELLS = 786432


def z_matrix():
    row = lax.broadcasted_iota(jnp.int32, (128, 128), 0)
    col = lax.broadcasted_iota(jnp.int32, (128, 128), 1)
    same = (row >= NZ) == (col >= NZ)
    apart = (row - col) & (NZ - 1)
    m = jnp.zeros((128, 128), F32)
    for k in range(1, 7):
        m = jnp.where(same & ((apart == k) | (apart == NZ - k)), A[k], m)
    hi = m.astype(BF)
    lo = (m - hi.astype(F32)).astype(BF)
    top = jnp.concatenate([hi, lo], axis=1)
    low = jnp.concatenate([hi, jnp.zeros_like(hi)], axis=1)
    return jnp.concatenate([top, low], axis=0)


def hamiltonian(src, planes, pots, w, ext):
    xs = [src[i] for i in planes]
    lhs = []
    for x in xs:
        t = jnp.concatenate([x[:, c * 128 : (c + 1) * 128] for c in range(16)], axis=0)
        hi = t.astype(BF)
        lo = (t - hi.astype(F32)).astype(BF)
        lhs.append(jnp.concatenate([hi, lo], axis=1))
    z = jnp.dot(jnp.concatenate(lhs, axis=0), w[...], preferred_element_type=F32)
    z = z[:, :128] + z[:, 128:]
    outs = []
    for j, (i, x) in enumerate(zip(planes, xs)):
        turned = pltpu.roll(x, NZ, 1)
        for e, v in ((0, x), (1, turned)):
            ext[j, e, :, EXT : EXT + PLANE] = v
            ext[j, e, :, :EXT] = v[:, PLANE - EXT :]
            ext[j, e, :, EXT + PLANE :] = v[:, :EXT]

        def along_y(k):
            odd = k % 2
            start = EXT + NZ * (k + odd)
            return ext[j, odd, :, start : start + PLANE]

        acc = (3 * A[0] + pots[j]) * x
        acc = acc + jnp.concatenate(
            [z[j * 128 + c * 8 : j * 128 + c * 8 + 8] for c in range(16)], axis=1
        )
        for k in range(1, 7):
            acc = acc + A[k] * (
                (src[i + k] + src[i - k]) + (along_y(k) + along_y(-k))
            )
        outs.append(acc)
    return xs, outs


def kernel(
    orb_hbm, pot, sub_hbm, corr, proj,
    orbs, own16, left16, right16, first, second, fleft, fright, rows16, pots, ext, w,
    sub, even, odd, squares, msg, got,
    s_loc, s_sub, s_toright, s_toleft, r_left, r_right, s_pot, r_pot,
    s_fright, s_fleft, r_fleft, r_fright,
    s_z, r_z, s_c, r_c, s_f, r_f, s_all, r_all,
):
    d = lax.axis_index("dom")
    b = lax.axis_index("orb")
    right = (lax.rem(d + 1, DOM), b)
    left = (lax.rem(d + DOM - 1, DOM), b)
    b_z = lax.rem(b + 2, 4)
    b_c = b + 1 - 2 * lax.rem(b, 2)
    b_zc = lax.rem(b_c + 2, 4)

    barrier = pltpu.get_barrier_semaphore()

    def greet(k, carry):
        pl.semaphore_signal(
            barrier, inc=1, device_id=(lax.rem(d + k, DOM), b), device_id_type=MESH
        )
        return carry

    lax.fori_loop(1, DOM, greet, 0)
    for peer in (b_z, b_c, b_zc):
        pl.semaphore_signal(barrier, inc=1, device_id=(d, peer), device_id_type=MESH)

    load = pltpu.make_async_copy(orb_hbm, orbs.at[pl.ds(12, 12)], s_loc)
    load.start()

    def load_sub(p):
        return pltpu.make_async_copy(sub_hbm.at[p], sub.at[p], s_sub.at[p])

    def start_sub(p, carry):
        load_sub(p).start()
        return carry

    lax.fori_loop(0, 12, start_sub, 0)
    w[...] = z_matrix()
    for p in range(12):
        pots[6 + p] = pot[p : p + 1, :]
    load.wait()

    def narrow(q, carry):
        own16[q] = jnp.concatenate([orbs[12 + 2 * q], orbs[13 + 2 * q]], axis=0).astype(BF)
        return carry

    lax.fori_loop(0, 6, narrow, 0)

    def remote(src, dst, ss, rs, device):
        return pltpu.make_async_remote_copy(
            src_ref=src, dst_ref=dst, send_sem=ss, recv_sem=rs,
            device_id=device, device_id_type=MESH,
        )

    def orb_right(q):
        return remote(own16.at[q], left16.at[q], s_toright.at[q], r_left.at[q], right)

    def orb_left(q):
        return remote(own16.at[q], right16.at[q], s_toleft.at[q], r_right.at[q], left)

    pot_right = remote(
        pots.at[pl.ds(12, 6)], pots.at[pl.ds(0, 6)], s_pot.at[0], r_pot.at[0], right
    )
    pot_left = remote(
        pots.at[pl.ds(6, 6)], pots.at[pl.ds(18, 6)], s_pot.at[1], r_pot.at[1], left
    )

    pl.semaphore_wait(barrier, DOM - 1 + 3)

    def send_orbs(j, carry):
        orb_right(5 - j).start()
        orb_left(j).start()
        return carry

    lax.fori_loop(0, 3, send_orbs, 0)
    pot_right.start()
    pot_left.start()
    lax.fori_loop(3, 6, send_orbs, 0)

    def widen(src, q, dst, at):
        both = src[q].astype(F32)
        dst[at] = both[:8]
        dst[at + 1] = both[8:]

    def take_orbs(j, carry):
        orb_right(5 - j).wait_recv()
        widen(left16, 5 - j, orbs, 2 * (5 - j))
        orb_left(j).wait_recv()
        widen(right16, j, orbs, 24 + 2 * j)
        return carry

    lax.fori_loop(0, 3, take_orbs, 0)

    def first_of(planes):
        xs, hs = hamiltonian(
            orbs, [p + 12 for p in planes], [pots[p + 6] for p in planes], w, ext
        )
        for p, x, h in zip(planes, xs, hs):
            first[p + 6] = 0.125 * h - x

    def inner(g, carry):
        first_of([g * GROUP + j for j in range(GROUP)])
        return carry

    lax.fori_loop(0, 3, inner, 0)
    pot_right.wait_recv()
    pot_left.wait_recv()

    def to_z(a, q):
        n = a * 6 + q
        return remote(
            rows16.at[a, b, q], rows16.at[a, b, q], s_z.at[n], r_z.at[n], (d, b_z)
        )

    def to_c(a, q):
        n = a * 6 + q
        return remote(
            rows16.at[a, b, q], rows16.at[a, b, q], s_c.at[n], r_c.at[n], (d, b_c)
        )

    def forward(a, q):
        n = a * 6 + q
        return remote(
            rows16.at[a, b_z, q], rows16.at[a, b_z, q], s_f.at[n], r_f.at[n], (d, b_c)
        )

    def come_z(a, q):
        n = a * 6 + q
        return remote(
            rows16.at[a, b_z, q], rows16.at[a, b_z, q], s_z.at[n], r_z.at[n], (d, b_z)
        )

    def come_c(a, q):
        n = a * 6 + q
        return remote(
            rows16.at[a, b_c, q], rows16.at[a, b_c, q], s_c.at[n], r_c.at[n], (d, b_c)
        )

    def come_f(a, q):
        n = a * 6 + q
        return remote(
            rows16.at[a, b_zc, q], rows16.at[a, b_zc, q], s_f.at[n], r_f.at[n], (d, b_c)
        )

    def filt_right(j):
        return remote(
            rows16.at[0, b, 3 + j], fleft.at[j], s_fright.at[j], r_fleft.at[j], right
        )

    def filt_left(j):
        return remote(
            rows16.at[0, b, j], fright.at[j], s_fleft.at[j], r_fright.at[j], left
        )

    def outer(s, carry):
        take_orbs(3 + s, 0)
        first_of([-2 - 2 * s, -1 - 2 * s, 12 + 2 * s, 13 + 2 * s])
        planes = [4 - 2 * s, 5 - 2 * s, 6 + 2 * s, 7 + 2 * s]
        xs, hs = hamiltonian(
            first, [p + 6 for p in planes], [pots[p + 6] for p in planes], w, ext
        )
        out = []
        for p, x, h in zip(planes, xs, hs):
            v = 0.25 * h - 2.0 * x - orbs[p + 12]
            second[p + 6] = v
            out.append(v)
        rows16[0, b, 2 - s] = jnp.concatenate(out[:2], axis=0).astype(BF)
        rows16[0, b, 3 + s] = jnp.concatenate(out[2:], axis=0).astype(BF)
        filt_left(2 - s).start()
        filt_right(s).start()
        to_z(0, 2 - s).start()
        to_z(0, 3 + s).start()
        to_c(0, 2 - s).start()
        to_c(0, 3 + s).start()
        return carry

    lax.fori_loop(0, 3, outer, 0)

    def pass_on(s, carry):
        come_z(0, 2 - s).wait_recv()
        forward(0, 2 - s).start()
        come_z(0, 3 + s).wait_recv()
        forward(0, 3 + s).start()
        return carry

    lax.fori_loop(0, 2, pass_on, 0)

    def take_filt(j, carry):
        filt_right(j).wait_recv()
        widen(fleft, j, second, 2 * j)
        filt_left(2 - j).wait_recv()
        widen(fright, 2 - j, second, 18 + 2 * (2 - j))
        return carry

    lax.fori_loop(0, 3, take_filt, 0)

    def last(g, carry):
        planes = [g * GROUP + j for j in range(GROUP)]
        _, hs = hamiltonian(
            second, [p + 6 for p in planes], [pots[p + 6] for p in planes], w, ext
        )
        rows16[1, b, 2 * g] = jnp.concatenate(hs[:2], axis=0).astype(BF)
        rows16[1, b, 2 * g + 1] = jnp.concatenate(hs[2:], axis=0).astype(BF)
        for q in (2 * g, 2 * g + 1):
            to_z(1, q).start()
            to_c(1, q).start()
        return carry

    lax.fori_loop(0, 3, last, 0)
    pass_on(2, 0)

    even[...] = jnp.zeros_like(even)
    odd[...] = jnp.zeros_like(odd)
    squares[...] = jnp.zeros_like(squares)

    def come_on(q):
        come_z(1, q).wait_recv()
        forward(1, q).start()

    def gram(q):
        for a in range(2):
            come_c(a, q).wait_recv()
            come_f(a, q).wait_recv()
        load_sub(2 * q).wait()
        load_sub(2 * q + 1).wait()
        filt = jnp.concatenate([rows16[0, o, q] for o in range(4)], axis=0)
        appl = jnp.concatenate([rows16[1, o, q] for o in range(4)], axis=0)
        rows = jnp.concatenate([filt, appl], axis=0)
        nt = (((1,), (1,)), ((), ()))
        even[...] += lax.dot_general(sub[2 * q], rows, nt, preferred_element_type=F32)
        odd[...] += lax.dot_general(sub[2 * q + 1], rows, nt, preferred_element_type=F32)
        total = squares[...]
        for c in range(16):
            x = filt[:, c * 128 : (c + 1) * 128].astype(F32)
            total = total + x * x
        squares[...] = total

    come_on(0)

    def step(q, carry):
        come_on(q + 1)
        gram(q)
        return carry

    lax.fori_loop(0, 5, step, 0)
    gram(5)

    from_even = even[...].T
    from_odd = odd[...].T
    sq = squares[...]
    for o in range(4):
        for a in range(2):
            at = a * 64 + o * 16
            block = from_even[at : at + 8] + from_odd[at + 8 : at + 16]
            for c in range(4):
                msg[pl.ds(o * 128 + a * 4 + c, 8, stride=16), :] = block[
                    :, c * 128 : (c + 1) * 128
                ]
        msg[pl.ds(o * 128 + 8, 8, stride=16), :] = sq[o * 16 : o * 16 + 8] + sq[o * 16 + 8 : o * 16 + 16]

    def to_all(k):
        t = lax.rem(d + k, DOM)
        return remote(
            msg.at[pl.ds(t * 16, 16)], got.at[pl.ds(d * 16, 16)],
            s_all.at[k - 1], r_all.at[k - 1], (t, b),
        )

    def from_all(k):
        t = lax.rem(d + DOM - k, DOM)
        return remote(
            msg.at[pl.ds(t * 16, 16)], got.at[pl.ds(t * 16, 16)],
            s_all.at[k - 1], r_all.at[k - 1], (t, b),
        )

    def send_all(k, carry):
        to_all(k).start()
        return carry

    lax.fori_loop(1, DOM, send_all, 0)
    got[pl.ds(d * 16, 16), :] = msg[pl.ds(d * 16, 16), :]

    def wait_sends(j, carry):
        orb_right(j).wait_send()
        orb_left(j).wait_send()
        for a in range(2):
            to_z(a, j).wait_send()
            to_c(a, j).wait_send()
            forward(a, j).wait_send()
        return carry

    lax.fori_loop(0, 6, wait_sends, 0)

    def wait_filt(j, carry):
        filt_right(j).wait_send()
        filt_left(j).wait_send()
        return carry

    lax.fori_loop(0, 3, wait_filt, 0)
    pot_right.wait_send()
    pot_left.wait_send()

    def wait_all(k, carry):
        from_all(k).wait_recv()
        return carry

    lax.fori_loop(1, DOM, wait_all, 0)
    total = got[pl.ds(0, 16), :]
    for t in range(1, DOM):
        total = total + got[pl.ds(t * 16, 16), :]
    scale = jnp.sqrt(jnp.sum(total[8:9, :], axis=1, keepdims=True) / CELLS + 1e-06)
    total = total[:8] / scale
    for c in range(4):
        corr[:, c * 128 : (c + 1) * 128] = total[c : c + 1]
        proj[:, c * 128 : (c + 1) * 128] = total[4 + c : 5 + c]

    def wait_sent(k, carry):
        to_all(k).wait_send()
        return carry

    lax.fori_loop(1, DOM, wait_sent, 0)


def shards(orbitals, potential, subspace):
    dma = pltpu.SemaphoreType.DMA
    return pl.pallas_call(
        kernel,
        out_shape=[jax.ShapeDtypeStruct((1, 512), F32)] * 2,
        in_specs=[
            pl.BlockSpec(memory_space=pl.ANY),
            pl.BlockSpec(memory_space=pltpu.VMEM),
            pl.BlockSpec(memory_space=pl.ANY),
        ],
        out_specs=[pl.BlockSpec(memory_space=pltpu.VMEM)] * 2,
        scratch_shapes=[
            pltpu.VMEM((36, 8, PLANE), F32),
            pltpu.VMEM((6, 16, PLANE), BF),
            pltpu.VMEM((6, 16, PLANE), BF),
            pltpu.VMEM((6, 16, PLANE), BF),
            pltpu.VMEM((24, 8, PLANE), F32),
            pltpu.VMEM((24, 8, PLANE), F32),
            pltpu.VMEM((3, 16, PLANE), BF),
            pltpu.VMEM((3, 16, PLANE), BF),
            pltpu.VMEM((2, 4, 6, 16, PLANE), BF),
            pltpu.VMEM((24, 1, PLANE), F32),
            pltpu.VMEM((GROUP, 2, 8, PLANE + 2 * EXT), F32),
            pltpu.VMEM((256, 256), BF),
            pltpu.VMEM((12, 512, PLANE), BF),
            pltpu.VMEM((512, 128), F32),
            pltpu.VMEM((512, 128), F32),
            pltpu.VMEM((64, 128), F32),
            pltpu.VMEM((DOM * 16, 128), F32),
            pltpu.VMEM((DOM * 16, 128), F32),
            dma(()), dma((12,)),
            dma((6,)), dma((6,)), dma((6,)), dma((6,)), dma((2,)), dma((2,)),
            dma((3,)), dma((3,)), dma((3,)), dma((3,)),
            dma((12,)), dma((12,)), dma((12,)), dma((12,)), dma((12,)), dma((12,)),
            dma((DOM - 1,)), dma((DOM - 1,)),
        ],
        compiler_params=pltpu.CompilerParams(
            collective_id=0, has_side_effects=True, vmem_limit_bytes=48 * 2**20
        ),
    )(orbitals.transpose(1, 0, 2), potential, subspace.transpose(1, 0, 2))


def solution(mesh):
    placed = (P("orb", "dom", None), P("dom", None), P("orb", "dom", None))
    return jax.shard_map(
        shards,
        mesh=mesh,
        in_specs=placed,
        out_specs=(P("dom", "orb"), P("dom", "orb")),
        check_vma=False,
    )
```

```python
import jax
import jax.numpy as jnp
from jax import lax
from jax.experimental import pallas as pl
from jax.experimental.pallas import tpu as pltpu
from jax.sharding import PartitionSpec as P

BF = jnp.bfloat16
F32 = jnp.float32
MESH = pl.DeviceIdType.MESH

coeffs = (
    -5369.0 / 1800.0,
    12.0 / 7.0,
    -15.0 / 56.0,
    10.0 / 189.0,
    -1.0 / 112.0,
    2.0 / 1925.0,
    -1.0 / 16632.0,
)
A = [-0.5 * c for c in coeffs]

NZ = 64
PLANE = 2048
EXT = 384
GROUP = 4
DOM = 32
AROUND = 1
ORDER = (2, 3, 1, 4, 0, 5)
CELLS = 786432


def z_matrix():
    row = lax.broadcasted_iota(jnp.int32, (128, 128), 0)
    col = lax.broadcasted_iota(jnp.int32, (128, 128), 1)
    same = (row >= NZ) == (col >= NZ)
    apart = (row - col) & (NZ - 1)
    m = jnp.zeros((128, 128), F32)
    for k in range(1, 7):
        m = jnp.where(same & ((apart == k) | (apart == NZ - k)), A[k], m)
    hi = m.astype(BF)
    lo = (m - hi.astype(F32)).astype(BF)
    top = jnp.concatenate([hi, lo], axis=1)
    low = jnp.concatenate([hi, jnp.zeros_like(hi)], axis=1)
    return jnp.concatenate([top, low], axis=0)


def hamiltonian(src, planes, pots, w, ext):
    xs = [src[i] for i in planes]
    lhs = []
    for x in xs:
        t = jnp.concatenate([x[:, c * 128 : (c + 1) * 128] for c in range(16)], axis=0)
        hi = t.astype(BF)
        lo = (t - hi.astype(F32)).astype(BF)
        lhs.append(jnp.concatenate([hi, lo], axis=1))
    z = jnp.dot(jnp.concatenate(lhs, axis=0), w[...], preferred_element_type=F32)
    z = z[:, :128] + z[:, 128:]
    outs = []
    for j, (i, x) in enumerate(zip(planes, xs)):
        turned = pltpu.roll(x, NZ, 1)
        for e, v in ((0, x), (1, turned)):
            ext[j, e, :, EXT : EXT + PLANE] = v
            ext[j, e, :, :EXT] = v[:, PLANE - EXT :]
            ext[j, e, :, EXT + PLANE :] = v[:, :EXT]

        def along_y(k):
            odd = k % 2
            start = EXT + NZ * (k + odd)
            return ext[j, odd, :, start : start + PLANE]

        acc = (3 * A[0] + pots[j]) * x
        acc = acc + jnp.concatenate(
            [z[j * 128 + c * 8 : j * 128 + c * 8 + 8] for c in range(16)], axis=1
        )
        for k in range(1, 7):
            acc = acc + A[k] * (
                (src[i + k] + src[i - k]) + (along_y(k) + along_y(-k))
            )
        outs.append(acc)
    return xs, outs


def kernel(
    orb_hbm, pot_hbm, sub_hbm, corr, proj,
    pot, orbs, own16, left16, right16, first, second, applied, fleft, fright, rows16, relay, pots, ext, w,
    sub, even, odd, msg, got,
    s_pots, s_loc, s_sub, s_toright, s_toleft, r_left, r_right, s_pot, r_pot,
    s_fright, s_fleft, r_fleft, r_fright,
    s_z, r_z, s_c, r_c, s_f, r_f, s_relay, r_relay, s_all, r_all,
):
    d = lax.axis_index("dom")
    b = lax.axis_index("orb")
    right = (lax.rem(d + 1, DOM), b)
    left = (lax.rem(d + DOM - 1, DOM), b)
    b_z = lax.rem(b + 2, 4)
    b_c = b + 1 - 2 * lax.rem(b, 2)
    b_zc = lax.rem(b_c + 2, 4)
    x = lax.rem(d, 4)
    mate = d + 1 - 2 * lax.rem(x, 2)
    edge = (x == 0) | (x == 3)

    barrier = pltpu.get_barrier_semaphore()
    load = pltpu.make_async_copy(orb_hbm, orbs.at[pl.ds(12, 12)], s_loc)
    load.start()
    load_pot = pltpu.make_async_copy(pot_hbm, pot, s_pots)
    load_pot.start()

    def greet(k, carry):
        pl.semaphore_signal(
            barrier, inc=1, device_id=(lax.rem(d + k, DOM), b), device_id_type=MESH
        )
        return carry

    lax.fori_loop(1, DOM, greet, 0)
    for peer in ((d, b_z), (d, b_c), (d, b_zc), (mate, b_z)):
        pl.semaphore_signal(barrier, inc=1, device_id=peer, device_id_type=MESH)

    def load_sub(p):
        return pltpu.make_async_copy(sub_hbm.at[p], sub.at[p], s_sub.at[p])

    def start_sub(p, carry):
        load_sub(p).start()
        return carry

    lax.fori_loop(0, 12, start_sub, 0)
    w[...] = z_matrix()
    second[pl.ds(0, 6)] = jnp.zeros((6, 8, PLANE), F32)
    second[pl.ds(18, 6)] = jnp.zeros((6, 8, PLANE), F32)
    load_pot.wait()
    for p in range(12):
        pots[6 + p] = pot[p : p + 1, :]
    load.wait()

    def narrow(q, carry):
        own16[q] = jnp.concatenate([orbs[12 + 2 * q], orbs[13 + 2 * q]], axis=0).astype(BF)
        return carry

    lax.fori_loop(0, 6, narrow, 0)

    def remote(src, dst, ss, rs, device):
        return pltpu.make_async_remote_copy(
            src_ref=src, dst_ref=dst, send_sem=ss, recv_sem=rs,
            device_id=device, device_id_type=MESH,
        )

    def orb_right(q):
        return remote(own16.at[q], left16.at[q], s_toright.at[q], r_left.at[q], right)

    def orb_left(q):
        return remote(own16.at[q], right16.at[q], s_toleft.at[q], r_right.at[q], left)

    pot_right = remote(
        pots.at[pl.ds(12, 6)], pots.at[pl.ds(0, 6)], s_pot.at[0], r_pot.at[0], right
    )
    pot_left = remote(
        pots.at[pl.ds(6, 6)], pots.at[pl.ds(18, 6)], s_pot.at[1], r_pot.at[1], left
    )

    pl.semaphore_wait(barrier, DOM - 1 + 4)

    def send_orbs(j, carry):
        orb_right(5 - j).start()
        orb_left(j).start()
        return carry

    lax.fori_loop(0, 3, send_orbs, 0)
    pot_right.start()
    pot_left.start()
    lax.fori_loop(3, 6, send_orbs, 0)

    def widen(src, q, dst, at):
        both = src[q].astype(F32)
        dst[at] = both[:8]
        dst[at + 1] = both[8:]

    def take_orbs(j, carry):
        orb_right(5 - j).wait_recv()
        widen(left16, 5 - j, orbs, 2 * (5 - j))
        orb_left(j).wait_recv()
        widen(right16, j, orbs, 24 + 2 * j)
        return carry

    lax.fori_loop(0, 3, take_orbs, 0)

    def first_of(planes):
        xs, hs = hamiltonian(
            orbs, [p + 12 for p in planes], [pots[p + 6] for p in planes], w, ext
        )
        for p, x, h in zip(planes, xs, hs):
            first[p + 6] = 0.125 * h - x

    def inner(g, carry):
        first_of([g * GROUP + j for j in range(GROUP)])
        return carry

    lax.fori_loop(0, 3, inner, 0)
    pot_right.wait_recv()
    pot_left.wait_recv()

    def to_z(a, q):
        n = a * 6 + q
        return remote(
            rows16.at[a, b, q], rows16.at[a, b, q], s_z.at[n], r_z.at[n], (d, b_z)
        )

    def to_c(a, q):
        n = a * 6 + q
        return remote(
            rows16.at[a, b, q], rows16.at[a, b, q], s_c.at[n], r_c.at[n], (d, b_c)
        )

    def forward(a, q):
        n = a * 6 + q
        return remote(
            rows16.at[a, b_z, q], rows16.at[a, b_z, q], s_f.at[n], r_f.at[n], (d, b_c)
        )

    def come_z(a, q):
        n = a * 6 + q
        return remote(
            rows16.at[a, b_z, q], rows16.at[a, b_z, q], s_z.at[n], r_z.at[n], (d, b_z)
        )

    def come_c(a, q):
        n = a * 6 + q
        return remote(
            rows16.at[a, b_c, q], rows16.at[a, b_c, q], s_c.at[n], r_c.at[n], (d, b_c)
        )

    def come_f(a, q):
        n = a * 6 + q
        return remote(
            rows16.at[a, b_zc, q], rows16.at[a, b_zc, q], s_f.at[n], r_f.at[n], (d, b_c)
        )

    def to_mate(q):
        return remote(
            rows16.at[0, b, q], relay.at[q], s_z.at[q], r_relay.at[q], (mate, b_z)
        )

    def from_mate(q):
        return remote(
            relay.at[q], rows16.at[0, b_z, q], s_relay.at[q], r_z.at[q], (mate, b)
        )

    def filt_right(j):
        return remote(
            rows16.at[0, b, 3 + j], fleft.at[j], s_fright.at[j], r_fleft.at[j], right
        )

    def filt_left(j):
        return remote(
            rows16.at[0, b, j], fright.at[j], s_fleft.at[j], r_fright.at[j], left
        )

    def outer(s, carry):
        take_orbs(3 + s, 0)
        first_of([-2 - 2 * s, -1 - 2 * s, 12 + 2 * s, 13 + 2 * s])
        planes = [4 - 2 * s, 5 - 2 * s, 6 + 2 * s, 7 + 2 * s]
        xs, hs = hamiltonian(
            first, [p + 6 for p in planes], [pots[p + 6] for p in planes], w, ext
        )
        out = []
        for p, x, h in zip(planes, xs, hs):
            v = 0.25 * h - 2.0 * x - orbs[p + 12]
            second[p + 6] = v
            out.append(v)
        rows16[0, b, 2 - s] = jnp.concatenate(out[:2], axis=0).astype(BF)
        rows16[0, b, 3 + s] = jnp.concatenate(out[2:], axis=0).astype(BF)
        filt_left(2 - s).start()
        filt_right(s).start()
        around = edge & (s < AROUND)

        @pl.when(around)
        def _():
            to_mate(2 - s).start()
            to_mate(3 + s).start()

        @pl.when(jnp.logical_not(around))
        def _():
            to_z(0, 2 - s).start()
            to_z(0, 3 + s).start()

        to_c(0, 2 - s).start()
        to_c(0, 3 + s).start()
        return carry

    lax.fori_loop(0, 3, outer, 0)

    def pass_on(s, carry):
        come_z(0, 2 - s).wait_recv()
        forward(0, 2 - s).start()
        come_z(0, 3 + s).wait_recv()
        forward(0, 3 + s).start()
        return carry

    def local(g, carry):
        planes = [g * GROUP + j for j in range(GROUP)]
        _, hs = hamiltonian(
            second, [p + 6 for p in planes], [pots[p + 6] for p in planes], w, ext
        )
        for p, h in zip(planes, hs):
            applied[p] = h
        return carry

    lax.fori_loop(0, 3, local, 0)

    def add_halo(j):
        filt_right(j).wait_recv()
        filt_left(2 - j).wait_recv()
        from_left = fleft[j].astype(F32)
        from_right = fright[2 - j].astype(F32)
        near, far = 5 - 2 * j, 6 - 2 * j
        for p in range(7 - near):
            low = A[near + p] * from_left[8:]
            high = A[near + p] * from_right[:8]
            if p <= 6 - far:
                low = low + A[far + p] * from_left[:8]
                high = high + A[far + p] * from_right[8:]
            applied[p] += low
            applied[11 - p] += high

    @pl.when(jnp.logical_not(edge))
    def _():
        for q in ORDER[: 2 * AROUND]:
            to_mate(q).wait_recv()
            from_mate(q).start()

    add_halo(0)
    add_halo(1)
    pass_on(0, 0)
    pass_on(1, 0)
    add_halo(2)
    for q in ORDER:
        rows16[1, b, q] = jnp.concatenate([applied[2 * q], applied[2 * q + 1]], axis=0).astype(BF)
        to_z(1, q).start()
        to_c(1, q).start()
    pass_on(2, 0)

    even[...] = jnp.zeros_like(even)
    odd[...] = jnp.zeros_like(odd)

    def come_on(q):
        come_z(1, q).wait_recv()
        forward(1, q).start()

    def gram(q, total):
        for a in range(2):
            come_c(a, q).wait_recv()
            come_f(a, q).wait_recv()
        load_sub(2 * q).wait()
        load_sub(2 * q + 1).wait()
        filt = jnp.concatenate([rows16[0, o, q] for o in range(4)], axis=0)
        appl = jnp.concatenate([rows16[1, o, q] for o in range(4)], axis=0)
        rows = jnp.concatenate([filt, appl], axis=0)
        nt = (((1,), (1,)), ((), ()))
        even[...] += lax.dot_general(sub[2 * q], rows, nt, preferred_element_type=F32)
        odd[...] += lax.dot_general(sub[2 * q + 1], rows, nt, preferred_element_type=F32)
        for c in range(16):
            v = filt[:, c * 128 : (c + 1) * 128].astype(F32)
            total = total + v * v
        return total

    def step(s, total):
        q = 2 - s // 2 + lax.rem(s, 2) * (2 * (s // 2) + 1)
        after = s + 1
        come_on(2 - after // 2 + lax.rem(after, 2) * (2 * (after // 2) + 1))
        return gram(q, total)

    come_on(2)
    squares = lax.fori_loop(0, 5, step, jnp.zeros((64, 128), F32))
    squares = gram(5, squares)

    from_even = even[...].T
    from_odd = odd[...].T
    for o in range(4):
        for a in range(2):
            at = a * 64 + o * 16
            block = from_even[at : at + 8] + from_odd[at + 8 : at + 16]
            for c in range(4):
                msg[pl.ds(o * 8, 8), a * 4 + c, :] = block[:, c * 128 : (c + 1) * 128]
        msg[pl.ds(o * 8, 8), 8, :] = squares[o * 16 : o * 16 + 8] + squares[o * 16 + 8 : o * 16 + 16]

    def to_all(k):
        t = lax.rem(d + k, DOM)
        return remote(msg.at[t], got.at[d], s_all.at[k], r_all.at[k], (t, b))

    def from_all(k):
        t = lax.rem(d + DOM - k, DOM)
        return remote(msg.at[t], got.at[t], s_all.at[k], r_all.at[k], (t, b))

    for k in sorted(range(1, DOM), key=lambda k: abs(k - DOM // 2)):
        to_all(k).start()
    got[d] = msg[d]

    def wait_sends(j, carry):
        orb_right(j).wait_send()
        orb_left(j).wait_send()
        for a in range(2):
            to_z(a, j).wait_send()
            to_c(a, j).wait_send()
            forward(a, j).wait_send()
        return carry

    lax.fori_loop(0, 6, wait_sends, 0)

    def wait_filt(j, carry):
        filt_right(j).wait_send()
        filt_left(j).wait_send()
        return carry

    lax.fori_loop(0, 3, wait_filt, 0)
    @pl.when(jnp.logical_not(edge))
    def _():
        for q in ORDER[: 2 * AROUND]:
            from_mate(q).wait_send()

    pot_right.wait_send()
    pot_left.wait_send()

    for k in range(1, DOM):
        to_all(k).wait_send()
    for k in range(1, DOM):
        from_all(k).wait_recv()
    total = got[0]
    for t in range(1, DOM):
        total = total + got[t]
    scale = jnp.sqrt(jnp.sum(total[8:], axis=1, keepdims=True) / CELLS + 1e-06)
    total = total[:8] / scale
    for c in range(4):
        corr[:, c * 128 : (c + 1) * 128] = total[c : c + 1]
        proj[:, c * 128 : (c + 1) * 128] = total[4 + c : 5 + c]


def shards(orbitals, potential, subspace):
    dma = pltpu.SemaphoreType.DMA
    return pl.pallas_call(
        kernel,
        out_shape=[jax.ShapeDtypeStruct((1, 512), F32)] * 2,
        in_specs=[
            pl.BlockSpec(memory_space=pltpu.HBM),
            pl.BlockSpec(memory_space=pltpu.HBM),
            pl.BlockSpec(memory_space=pltpu.HBM),
        ],
        out_specs=[pl.BlockSpec(memory_space=pltpu.VMEM)] * 2,
        scratch_shapes=[
            pltpu.VMEM((12, PLANE), F32),
            pltpu.VMEM((36, 8, PLANE), F32),
            pltpu.VMEM((6, 16, PLANE), BF),
            pltpu.VMEM((6, 16, PLANE), BF),
            pltpu.VMEM((6, 16, PLANE), BF),
            pltpu.VMEM((24, 8, PLANE), F32),
            pltpu.VMEM((24, 8, PLANE), F32),
            pltpu.VMEM((12, 8, PLANE), F32),
            pltpu.VMEM((3, 16, PLANE), BF),
            pltpu.VMEM((3, 16, PLANE), BF),
            pltpu.VMEM((2, 4, 6, 16, PLANE), BF),
            pltpu.VMEM((6, 16, PLANE), BF),
            pltpu.VMEM((24, 1, PLANE), F32),
            pltpu.VMEM((GROUP, 2, 8, PLANE + 2 * EXT), F32),
            pltpu.VMEM((256, 256), BF),
            pltpu.VMEM((12, 512, PLANE), BF),
            pltpu.VMEM((512, 128), F32),
            pltpu.VMEM((512, 128), F32),
            pltpu.VMEM((DOM, 9, 128), F32),
            pltpu.VMEM((DOM, 9, 128), F32),
            dma(()), dma(()), dma((12,)),
            dma((6,)), dma((6,)), dma((6,)), dma((6,)), dma((2,)), dma((2,)),
            dma((3,)), dma((3,)), dma((3,)), dma((3,)),
            dma((12,)), dma((12,)), dma((12,)), dma((12,)), dma((12,)), dma((12,)),
            dma((6,)), dma((6,)), dma((DOM,)), dma((DOM,)),
        ],
        compiler_params=pltpu.CompilerParams(
            collective_id=0, has_side_effects=True, vmem_limit_bytes=64 * 2**20 - 10400 * 1024
        ),
    )(orbitals.transpose(1, 0, 2), potential, subspace.transpose(1, 0, 2))


def solution(mesh):
    placed = (P("orb", "dom", None), P("dom", None), P("orb", "dom", None))
    return jax.shard_map(
        shards,
        mesh=mesh,
        in_specs=placed,
        out_specs=(P("dom", "orb"), P("dom", "orb")),
        check_vma=False,
    )
```

```python
import jax
import jax.numpy as jnp
from jax import lax
from jax.experimental import pallas as pl
from jax.experimental.pallas import tpu as pltpu
from jax.sharding import PartitionSpec as P

BF = jnp.bfloat16
F32 = jnp.float32
MESH = pl.DeviceIdType.MESH

coeffs = (
    -5369.0 / 1800.0,
    12.0 / 7.0,
    -15.0 / 56.0,
    10.0 / 189.0,
    -1.0 / 112.0,
    2.0 / 1925.0,
    -1.0 / 16632.0,
)
A = [-0.5 * c for c in coeffs]

NZ = 64
PLANE = 2048
EXT = 384
GROUP = 4
DOM = 32
AROUND = 1
ORDER = (2, 3, 1, 4, 0, 5)
CELLS = 786432


def z_matrix():
    row = lax.broadcasted_iota(jnp.int32, (128, 128), 0)
    col = lax.broadcasted_iota(jnp.int32, (128, 128), 1)
    same = (row >= NZ) == (col >= NZ)
    apart = (row - col) & (NZ - 1)
    m = jnp.zeros((128, 128), F32)
    for k in range(1, 7):
        m = jnp.where(same & ((apart == k) | (apart == NZ - k)), A[k], m)
    hi = m.astype(BF)
    lo = (m - hi.astype(F32)).astype(BF)
    top = jnp.concatenate([hi, lo], axis=1)
    low = jnp.concatenate([hi, jnp.zeros_like(hi)], axis=1)
    return jnp.concatenate([top, low], axis=0)


def hamiltonian(src, planes, pots, w, ext):
    xs = [src[i] for i in planes]
    lhs = []
    for x in xs:
        t = jnp.concatenate([x[:, c * 128 : (c + 1) * 128] for c in range(16)], axis=0)
        hi = t.astype(BF)
        lo = (t - hi.astype(F32)).astype(BF)
        lhs.append(jnp.concatenate([hi, lo], axis=1))
    z = jnp.dot(jnp.concatenate(lhs, axis=0), w[...], preferred_element_type=F32)
    z = z[:, :128] + z[:, 128:]
    outs = []
    for j, (i, x) in enumerate(zip(planes, xs)):
        turned = pltpu.roll(x, NZ, 1)
        for e, v in ((0, x), (1, turned)):
            ext[j, e, :, EXT : EXT + PLANE] = v
            ext[j, e, :, :EXT] = v[:, PLANE - EXT :]
            ext[j, e, :, EXT + PLANE :] = v[:, :EXT]

        def along_y(k):
            odd = k % 2
            start = EXT + NZ * (k + odd)
            return ext[j, odd, :, start : start + PLANE]

        acc = (3 * A[0] + pots[j]) * x
        acc = acc + jnp.concatenate(
            [z[j * 128 + c * 8 : j * 128 + c * 8 + 8] for c in range(16)], axis=1
        )
        for k in range(1, 7):
            acc = acc + A[k] * (
                (src[i + k] + src[i - k]) + (along_y(k) + along_y(-k))
            )
        outs.append(acc)
    return xs, outs


def kernel(
    orb_hbm, pot_hbm, sub_hbm, both,
    pot, orbs, own16, left16, right16, first, second, applied, fleft, fright, rows16, relay, pots, ext, w,
    sub, even, odd, msg, got,
    s_pots, s_loc, s_sub, s_toright, s_toleft, r_left, r_right, s_pot, r_pot, s_share, r_share,
    s_fright, s_fleft, r_fleft, r_fright,
    s_z, r_z, s_c, r_c, s_f, r_f, s_relay, r_relay, s_all, r_all,
):
    d = lax.axis_index("dom")
    b = lax.axis_index("orb")
    right = (lax.rem(d + 1, DOM), b)
    left = (lax.rem(d + DOM - 1, DOM), b)
    b_z = lax.rem(b + 2, 4)
    b_c = b + 1 - 2 * lax.rem(b, 2)
    b_zc = lax.rem(b_c + 2, 4)
    x = lax.rem(d, 4)
    mate = d + 1 - 2 * lax.rem(x, 2)
    edge = (x == 0) | (x == 3)

    barrier = pltpu.get_barrier_semaphore()
    load = pltpu.make_async_copy(orb_hbm, orbs.at[pl.ds(12, 12)], s_loc)
    load.start()
    load_pot = pltpu.make_async_copy(pot_hbm, pot, s_pots)
    load_pot.start()

    def greet(k, carry):
        pl.semaphore_signal(
            barrier, inc=1, device_id=(lax.rem(d + k, DOM), b), device_id_type=MESH
        )
        return carry

    lax.fori_loop(1, DOM, greet, 0)
    for peer in ((d, b_z), (d, b_c), (d, b_zc), (mate, b_z)):
        pl.semaphore_signal(barrier, inc=1, device_id=peer, device_id_type=MESH)

    def load_sub(p):
        return pltpu.make_async_copy(sub_hbm.at[p], sub.at[p], s_sub.at[p])

    def start_sub(p, carry):
        load_sub(p).start()
        return carry

    lax.fori_loop(0, 12, start_sub, 0)
    load_pot.wait()
    for p in range(12):
        pots[6 + p] = pot[p : p + 1, :]
    load.wait()

    def narrow(q, carry):
        own16[q] = jnp.concatenate([orbs[12 + 2 * q], orbs[13 + 2 * q]], axis=0).astype(BF)
        return carry

    lax.fori_loop(0, 6, narrow, 0)

    def remote(src, dst, ss, rs, device):
        return pltpu.make_async_remote_copy(
            src_ref=src, dst_ref=dst, send_sem=ss, recv_sem=rs,
            device_id=device, device_id_type=MESH,
        )

    def orb_right(q):
        return remote(own16.at[q], left16.at[q], s_toright.at[q], r_left.at[q], right)

    def orb_left(q):
        return remote(own16.at[q], right16.at[q], s_toleft.at[q], r_right.at[q], left)

    def half(start, o):
        at = pl.multiple_of(lax.rem(o, 2) * 1024, 1024)
        return pots.at[pl.ds(start, 6), :, pl.ds(at, 1024)]

    pot_right = remote(half(12, b), half(0, b), s_pot.at[0], r_pot.at[0], right)
    pot_left = remote(half(6, b), half(18, b), s_pot.at[1], r_pot.at[1], left)

    def share(side):
        mine = half(18 * side, b)
        return remote(mine, mine, s_share.at[side], r_share.at[side], (d, b_c))

    def shared(side):
        other = half(18 * side, b_c)
        return remote(other, other, s_share.at[side], r_share.at[side], (d, b_c))

    pl.semaphore_wait(barrier, DOM - 1 + 4)

    def send_orbs(j, carry):
        orb_right(5 - j).start()
        orb_left(j).start()
        return carry

    pot_right.start()
    pot_left.start()
    lax.fori_loop(0, 6, send_orbs, 0)

    def widen(src, q, dst, at):
        both = src[q].astype(F32)
        dst[at] = both[:8]
        dst[at + 1] = both[8:]

    def take_orbs(j, carry):
        orb_right(5 - j).wait_recv()
        widen(left16, 5 - j, orbs, 2 * (5 - j))
        orb_left(j).wait_recv()
        widen(right16, j, orbs, 24 + 2 * j)
        return carry

    w[...] = z_matrix()
    second[pl.ds(0, 6)] = jnp.zeros((6, 8, PLANE), F32)
    second[pl.ds(18, 6)] = jnp.zeros((6, 8, PLANE), F32)
    pot_right.wait_recv()
    share(0).start()
    pot_left.wait_recv()
    share(1).start()
    lax.fori_loop(0, 3, take_orbs, 0)

    def first_of(planes):
        xs, hs = hamiltonian(
            orbs, [p + 12 for p in planes], [pots[p + 6] for p in planes], w, ext
        )
        for p, x, h in zip(planes, xs, hs):
            first[p + 6] = 0.125 * h - x

    def inner(g, carry):
        first_of([g * GROUP + j for j in range(GROUP)])
        return carry

    lax.fori_loop(0, 3, inner, 0)
    shared(0).wait_recv()
    shared(1).wait_recv()

    def to_z(a, q):
        n = a * 6 + q
        return remote(
            rows16.at[a, b, q], rows16.at[a, b, q], s_z.at[n], r_z.at[n], (d, b_z)
        )

    def to_c(a, q):
        n = a * 6 + q
        return remote(
            rows16.at[a, b, q], rows16.at[a, b, q], s_c.at[n], r_c.at[n], (d, b_c)
        )

    def forward(a, q):
        n = a * 6 + q
        return remote(
            rows16.at[a, b_z, q], rows16.at[a, b_z, q], s_f.at[n], r_f.at[n], (d, b_c)
        )

    def come_z(a, q):
        n = a * 6 + q
        return remote(
            rows16.at[a, b_z, q], rows16.at[a, b_z, q], s_z.at[n], r_z.at[n], (d, b_z)
        )

    def come_c(a, q):
        n = a * 6 + q
        return remote(
            rows16.at[a, b_c, q], rows16.at[a, b_c, q], s_c.at[n], r_c.at[n], (d, b_c)
        )

    def come_f(a, q):
        n = a * 6 + q
        return remote(
            rows16.at[a, b_zc, q], rows16.at[a, b_zc, q], s_f.at[n], r_f.at[n], (d, b_c)
        )

    def to_mate(q):
        return remote(
            rows16.at[0, b, q], relay.at[q], s_z.at[q], r_relay.at[q], (mate, b_z)
        )

    def from_mate(q):
        return remote(
            relay.at[q], rows16.at[0, b_z, q], s_relay.at[q], r_z.at[q], (mate, b)
        )

    def filt_right(j):
        return remote(
            rows16.at[0, b, 3 + j], fleft.at[j], s_fright.at[j], r_fleft.at[j], right
        )

    def filt_left(j):
        return remote(
            rows16.at[0, b, j], fright.at[j], s_fleft.at[j], r_fright.at[j], left
        )

    def outer(s, carry):
        take_orbs(3 + s, 0)
        first_of([-2 - 2 * s, -1 - 2 * s, 12 + 2 * s, 13 + 2 * s])
        planes = [4 - 2 * s, 5 - 2 * s, 6 + 2 * s, 7 + 2 * s]
        xs, hs = hamiltonian(
            first, [p + 6 for p in planes], [pots[p + 6] for p in planes], w, ext
        )
        out = []
        for p, x, h in zip(planes, xs, hs):
            v = 0.25 * h - 2.0 * x - orbs[p + 12]
            second[p + 6] = v
            out.append(v)
        rows16[0, b, 2 - s] = jnp.concatenate(out[:2], axis=0).astype(BF)
        rows16[0, b, 3 + s] = jnp.concatenate(out[2:], axis=0).astype(BF)
        filt_left(2 - s).start()
        filt_right(s).start()
        around = edge & (s < AROUND)

        @pl.when(around)
        def _():
            to_mate(2 - s).start()
            to_mate(3 + s).start()

        @pl.when(jnp.logical_not(around))
        def _():
            to_z(0, 2 - s).start()
            to_z(0, 3 + s).start()

        to_c(0, 2 - s).start()
        to_c(0, 3 + s).start()
        return carry

    lax.fori_loop(0, 3, outer, 0)

    def pass_on(s, carry):
        come_z(0, 2 - s).wait_recv()
        forward(0, 2 - s).start()
        come_z(0, 3 + s).wait_recv()
        forward(0, 3 + s).start()
        return carry

    def local(g, carry):
        planes = [g * GROUP + j for j in range(GROUP)]
        _, hs = hamiltonian(
            second, [p + 6 for p in planes], [pots[p + 6] for p in planes], w, ext
        )
        for p, h in zip(planes, hs):
            applied[p] = h
        return carry

    lax.fori_loop(0, 3, local, 0)

    def add_halo(j):
        filt_right(j).wait_recv()
        filt_left(2 - j).wait_recv()
        from_left = fleft[j].astype(F32)
        from_right = fright[2 - j].astype(F32)
        near, far = 5 - 2 * j, 6 - 2 * j
        for p in range(7 - near):
            low = A[near + p] * from_left[8:]
            high = A[near + p] * from_right[:8]
            if p <= 6 - far:
                low = low + A[far + p] * from_left[:8]
                high = high + A[far + p] * from_right[8:]
            applied[p] += low
            applied[11 - p] += high

    @pl.when(jnp.logical_not(edge))
    def _():
        for q in ORDER[: 2 * AROUND]:
            to_mate(q).wait_recv()
            from_mate(q).start()

    add_halo(0)
    add_halo(1)
    pass_on(0, 0)
    pass_on(1, 0)
    add_halo(2)
    for q in ORDER:
        rows16[1, b, q] = jnp.concatenate([applied[2 * q], applied[2 * q + 1]], axis=0).astype(BF)
        to_z(1, q).start()
        to_c(1, q).start()
    pass_on(2, 0)

    even[...] = jnp.zeros_like(even)
    odd[...] = jnp.zeros_like(odd)

    def come_on(q):
        come_z(1, q).wait_recv()
        forward(1, q).start()

    def gram(q, total):
        for a in range(2):
            come_c(a, q).wait_recv()
            come_f(a, q).wait_recv()
        load_sub(2 * q).wait()
        load_sub(2 * q + 1).wait()
        filt = jnp.concatenate([rows16[0, o, q] for o in range(4)], axis=0)
        appl = jnp.concatenate([rows16[1, o, q] for o in range(4)], axis=0)
        rows = jnp.concatenate([filt, appl], axis=0)
        nt = (((1,), (1,)), ((), ()))
        even[...] += lax.dot_general(sub[2 * q], rows, nt, preferred_element_type=F32)
        odd[...] += lax.dot_general(sub[2 * q + 1], rows, nt, preferred_element_type=F32)
        for c in range(16):
            v = filt[:, c * 128 : (c + 1) * 128].astype(F32)
            total = total + v * v
        return total

    def step(s, total):
        q = 2 - s // 2 + lax.rem(s, 2) * (2 * (s // 2) + 1)
        after = s + 1
        come_on(2 - after // 2 + lax.rem(after, 2) * (2 * (after // 2) + 1))
        return gram(q, total)

    come_on(2)
    squares = lax.fori_loop(0, 5, step, jnp.zeros((64, 128), F32))
    squares = gram(5, squares)

    from_even = even[...].T
    from_odd = odd[...].T
    for o in range(4):
        for a in range(2):
            at = a * 64 + o * 16
            block = from_even[at : at + 8] + from_odd[at + 8 : at + 16]
            for c in range(4):
                msg[pl.ds(o * 8, 8), a * 4 + c, :] = block[:, c * 128 : (c + 1) * 128]
        msg[pl.ds(o * 8, 8), 8, :] = squares[o * 16 : o * 16 + 8] + squares[o * 16 + 8 : o * 16 + 16]

    def to_all(k):
        t = lax.rem(d + k, DOM)
        return remote(msg.at[t], got.at[d], s_all.at[k], r_all.at[k], (t, b))

    def from_all(k):
        t = lax.rem(d + DOM - k, DOM)
        return remote(msg.at[t], got.at[t], s_all.at[k], r_all.at[k], (t, b))

    for k in sorted(range(1, DOM), key=lambda k: abs(k - DOM // 2)):
        to_all(k).start()
    got[d] = msg[d]

    def wait_sends(j, carry):
        orb_right(j).wait_send()
        orb_left(j).wait_send()
        for a in range(2):
            to_z(a, j).wait_send()
            to_c(a, j).wait_send()
            forward(a, j).wait_send()
        return carry

    lax.fori_loop(0, 6, wait_sends, 0)

    def wait_filt(j, carry):
        filt_right(j).wait_send()
        filt_left(j).wait_send()
        return carry

    lax.fori_loop(0, 3, wait_filt, 0)
    @pl.when(jnp.logical_not(edge))
    def _():
        for q in ORDER[: 2 * AROUND]:
            from_mate(q).wait_send()

    pot_right.wait_send()
    pot_left.wait_send()
    share(0).wait_send()
    share(1).wait_send()

    for k in range(1, DOM):
        to_all(k).wait_send()
    for k in range(1, DOM):
        from_all(k).wait_recv()
    total = got[0]
    for t in range(1, DOM):
        total = total + got[t]
    scale = jnp.sqrt(jnp.sum(total[8:], axis=1, keepdims=True) / CELLS + 1e-06)
    total = total[:8] / scale
    for c in range(4):
        both[0:1, c * 128 : (c + 1) * 128] = total[c : c + 1]
        both[1:2, c * 128 : (c + 1) * 128] = total[4 + c : 5 + c]


def shards(orbitals, potential, subspace):
    dma = pltpu.SemaphoreType.DMA
    both = pl.pallas_call(
        kernel,
        out_shape=jax.ShapeDtypeStruct((2, 512), F32),
        in_specs=[
            pl.BlockSpec(memory_space=pltpu.HBM),
            pl.BlockSpec(memory_space=pltpu.HBM),
            pl.BlockSpec(memory_space=pltpu.HBM),
        ],
        out_specs=pl.BlockSpec(memory_space=pltpu.VMEM),
        scratch_shapes=[
            pltpu.VMEM((12, PLANE), F32),
            pltpu.VMEM((36, 8, PLANE), F32),
            pltpu.VMEM((6, 16, PLANE), BF),
            pltpu.VMEM((6, 16, PLANE), BF),
            pltpu.VMEM((6, 16, PLANE), BF),
            pltpu.VMEM((24, 8, PLANE), F32),
            pltpu.VMEM((24, 8, PLANE), F32),
            pltpu.VMEM((12, 8, PLANE), F32),
            pltpu.VMEM((3, 16, PLANE), BF),
            pltpu.VMEM((3, 16, PLANE), BF),
            pltpu.VMEM((2, 4, 6, 16, PLANE), BF),
            pltpu.VMEM((6, 16, PLANE), BF),
            pltpu.VMEM((24, 1, PLANE), F32),
            pltpu.VMEM((GROUP, 2, 8, PLANE + 2 * EXT), F32),
            pltpu.VMEM((256, 256), BF),
            pltpu.VMEM((12, 512, PLANE), BF),
            pltpu.VMEM((512, 128), F32),
            pltpu.VMEM((512, 128), F32),
            pltpu.VMEM((DOM, 9, 128), F32),
            pltpu.VMEM((DOM, 9, 128), F32),
            dma(()), dma(()), dma((12,)),
            dma((6,)), dma((6,)), dma((6,)), dma((6,)), dma((2,)), dma((2,)), dma((2,)), dma((2,)),
            dma((3,)), dma((3,)), dma((3,)), dma((3,)),
            dma((12,)), dma((12,)), dma((12,)), dma((12,)), dma((12,)), dma((12,)),
            dma((6,)), dma((6,)), dma((DOM,)), dma((DOM,)),
        ],
        compiler_params=pltpu.CompilerParams(
            collective_id=0, has_side_effects=True, vmem_limit_bytes=64 * 2**20 - 10400 * 1024
        ),
    )(orbitals.transpose(1, 0, 2), potential, subspace.transpose(1, 0, 2))
    return both[0:1], both[1:2]


def solution(mesh):
    placed = (P("orb", "dom", None), P("dom", None), P("orb", "dom", None))
    return jax.shard_map(
        shards,
        mesh=mesh,
        in_specs=placed,
        out_specs=(P("dom", "orb"), P("dom", "orb")),
        check_vma=False,
    )
```

```python
import jax
import jax.numpy as jnp
from jax import lax
from jax.experimental import pallas as pl
from jax.experimental.pallas import tpu as pltpu
from jax.sharding import PartitionSpec as P

BF = jnp.bfloat16
F32 = jnp.float32
MESH = pl.DeviceIdType.MESH

coeffs = (
    -5369.0 / 1800.0,
    12.0 / 7.0,
    -15.0 / 56.0,
    10.0 / 189.0,
    -1.0 / 112.0,
    2.0 / 1925.0,
    -1.0 / 16632.0,
)
A = [-0.5 * c for c in coeffs]

NZ = 64
PLANE = 2048
EXT = 384
GROUP = 4
DOM = 32
AROUND = 1
ORDER = (2, 3, 1, 4, 0, 5)
CELLS = 786432


def z_matrix():
    row = lax.broadcasted_iota(jnp.int32, (128, 128), 0)
    col = lax.broadcasted_iota(jnp.int32, (128, 128), 1)
    same = (row >= NZ) == (col >= NZ)
    apart = (row - col) & (NZ - 1)
    m = jnp.zeros((128, 128), F32)
    for k in range(1, 7):
        m = jnp.where(same & ((apart == k) | (apart == NZ - k)), A[k], m)
    hi = m.astype(BF)
    lo = (m - hi.astype(F32)).astype(BF)
    top = jnp.concatenate([hi, lo], axis=1)
    low = jnp.concatenate([hi, jnp.zeros_like(hi)], axis=1)
    return jnp.concatenate([top, low], axis=0)


def hamiltonian(src, planes, pots, w, ext):
    xs = [src[i] for i in planes]
    lhs = []
    for x in xs:
        t = jnp.concatenate([x[:, c * 128 : (c + 1) * 128] for c in range(16)], axis=0)
        hi = t.astype(BF)
        lo = (t - hi.astype(F32)).astype(BF)
        lhs.append(jnp.concatenate([hi, lo], axis=1))
    z = jnp.dot(jnp.concatenate(lhs, axis=0), w[...], preferred_element_type=F32)
    z = z[:, :128] + z[:, 128:]
    outs = []
    for j, (i, x) in enumerate(zip(planes, xs)):
        turned = pltpu.roll(x, NZ, 1)
        for e, v in ((0, x), (1, turned)):
            ext[j, e, :, EXT : EXT + PLANE] = v
            ext[j, e, :, :EXT] = v[:, PLANE - EXT :]
            ext[j, e, :, EXT + PLANE :] = v[:, :EXT]

        def along_y(k):
            odd = k % 2
            start = EXT + NZ * (k + odd)
            return ext[j, odd, :, start : start + PLANE]

        acc = (3 * A[0] + pots[j]) * x
        acc = acc + jnp.concatenate(
            [z[j * 128 + c * 8 : j * 128 + c * 8 + 8] for c in range(16)], axis=1
        )
        for k in range(1, 7):
            acc = acc + A[k] * (
                (src[i + k] + src[i - k]) + (along_y(k) + along_y(-k))
            )
        outs.append(acc)
    return xs, outs


def kernel(
    orb_hbm, pot_hbm, sub_hbm, both,
    pot, orbs, own16, left16, right16, first, second, applied, fleft, fright, rows16, relay, pots, ext, w,
    sub, even, odd, msg, got,
    row_in, plane_in, s_pots, s_loc, s_sub, s_toright, s_toleft, r_left, r_right, s_pot, r_pot, s_share, r_share,
    s_fright, s_fleft, r_fleft, r_fright,
    s_z, r_z, s_c, r_c, s_f, r_f, s_relay, r_relay, s_all, r_all,
):
    d = lax.axis_index("dom")
    b = lax.axis_index("orb")
    right = (lax.rem(d + 1, DOM), b)
    left = (lax.rem(d + DOM - 1, DOM), b)
    b_z = lax.rem(b + 2, 4)
    b_c = b + 1 - 2 * lax.rem(b, 2)
    b_zc = lax.rem(b_c + 2, 4)
    x = lax.rem(d, 4)
    mate = d + 1 - 2 * lax.rem(x, 2)
    edge = (x == 0) | (x == 3)

    barrier = pltpu.get_barrier_semaphore()
    load = pltpu.make_async_copy(orb_hbm, orbs.at[pl.ds(12, 12)], s_loc)
    load.start()
    load_pot = pltpu.make_async_copy(pot_hbm, pot, s_pots)
    load_pot.start()

    beyond = d + 4 - 8 * lax.rem(d // 4, 2)
    same_y = [d - x + lax.rem(x + k, 4) for k in range(1, 4)]
    across_y = [lax.rem(d + 8 * k, DOM) for k in range(1, 4)]
    peers_in = [right, left, (d, b_z), (d, b_c), (d, b_zc), (mate, b_z)]
    peers_in += [(t, b) for t in [*same_y, *across_y, beyond]]
    for peer in peers_in:
        pl.semaphore_signal(barrier, inc=1, device_id=peer, device_id_type=MESH)

    def load_sub(p):
        return pltpu.make_async_copy(sub_hbm.at[p], sub.at[p], s_sub.at[p])

    def start_sub(p, carry):
        load_sub(p).start()
        return carry

    lax.fori_loop(0, 12, start_sub, 0)
    load_pot.wait()
    for p in range(12):
        pots[6 + p] = pot[p : p + 1, :]
    load.wait()

    def narrow(q, carry):
        own16[q] = jnp.concatenate([orbs[12 + 2 * q], orbs[13 + 2 * q]], axis=0).astype(BF)
        return carry

    lax.fori_loop(0, 6, narrow, 0)

    def remote(src, dst, ss, rs, device):
        return pltpu.make_async_remote_copy(
            src_ref=src, dst_ref=dst, send_sem=ss, recv_sem=rs,
            device_id=device, device_id_type=MESH,
        )

    def orb_right(q):
        return remote(own16.at[q], left16.at[q], s_toright.at[q], r_left.at[q], right)

    def orb_left(q):
        return remote(own16.at[q], right16.at[q], s_toleft.at[q], r_right.at[q], left)

    def half(start, o):
        at = pl.multiple_of(lax.rem(o, 2) * 1024, 1024)
        return pots.at[pl.ds(start, 6), :, pl.ds(at, 1024)]

    pot_right = remote(half(12, b), half(0, b), s_pot.at[0], r_pot.at[0], right)
    pot_left = remote(half(6, b), half(18, b), s_pot.at[1], r_pot.at[1], left)

    def share(side):
        mine = half(18 * side, b)
        return remote(mine, mine, s_share.at[side], r_share.at[side], (d, b_c))

    def shared(side):
        other = half(18 * side, b_c)
        return remote(other, other, s_share.at[side], r_share.at[side], (d, b_c))

    pl.semaphore_wait(barrier, len(peers_in))

    def send_orbs(j, carry):
        orb_right(5 - j).start()
        orb_left(j).start()
        return carry

    pot_right.start()
    pot_left.start()
    lax.fori_loop(0, 6, send_orbs, 0)

    for t in across_y:
        pl.semaphore_signal(row_in, inc=1, device_id=(t, b), device_id_type=MESH)

    def widen(src, q, dst, at):
        both = src[q].astype(F32)
        dst[at] = both[:8]
        dst[at + 1] = both[8:]

    def take_orbs(j, carry):
        orb_right(5 - j).wait_recv()
        widen(left16, 5 - j, orbs, 2 * (5 - j))
        orb_left(j).wait_recv()
        widen(right16, j, orbs, 24 + 2 * j)
        return carry

    w[...] = z_matrix()
    second[pl.ds(0, 6)] = jnp.zeros((6, 8, PLANE), F32)
    second[pl.ds(18, 6)] = jnp.zeros((6, 8, PLANE), F32)
    pot_right.wait_recv()
    share(0).start()
    pot_left.wait_recv()
    share(1).start()
    lax.fori_loop(0, 3, take_orbs, 0)

    def first_of(planes):
        xs, hs = hamiltonian(
            orbs, [p + 12 for p in planes], [pots[p + 6] for p in planes], w, ext
        )
        for p, x, h in zip(planes, xs, hs):
            first[p + 6] = 0.125 * h - x

    def inner(g, carry):
        first_of([g * GROUP + j for j in range(GROUP)])
        return carry

    lax.fori_loop(0, 3, inner, 0)
    shared(0).wait_recv()
    shared(1).wait_recv()
    pl.semaphore_wait(row_in, len(across_y))
    pl.semaphore_signal(plane_in, inc=1, device_id=(beyond, b), device_id_type=MESH)

    def to_z(a, q):
        n = a * 6 + q
        return remote(
            rows16.at[a, b, q], rows16.at[a, b, q], s_z.at[n], r_z.at[n], (d, b_z)
        )

    def to_c(a, q):
        n = a * 6 + q
        return remote(
            rows16.at[a, b, q], rows16.at[a, b, q], s_c.at[n], r_c.at[n], (d, b_c)
        )

    def forward(a, q):
        n = a * 6 + q
        return remote(
            rows16.at[a, b_z, q], rows16.at[a, b_z, q], s_f.at[n], r_f.at[n], (d, b_c)
        )

    def come_z(a, q):
        n = a * 6 + q
        return remote(
            rows16.at[a, b_z, q], rows16.at[a, b_z, q], s_z.at[n], r_z.at[n], (d, b_z)
        )

    def come_c(a, q):
        n = a * 6 + q
        return remote(
            rows16.at[a, b_c, q], rows16.at[a, b_c, q], s_c.at[n], r_c.at[n], (d, b_c)
        )

    def come_f(a, q):
        n = a * 6 + q
        return remote(
            rows16.at[a, b_zc, q], rows16.at[a, b_zc, q], s_f.at[n], r_f.at[n], (d, b_c)
        )

    def to_mate(q):
        return remote(
            rows16.at[0, b, q], relay.at[q], s_z.at[q], r_relay.at[q], (mate, b_z)
        )

    def from_mate(q):
        return remote(
            relay.at[q], rows16.at[0, b_z, q], s_relay.at[q], r_z.at[q], (mate, b)
        )

    def filt_right(j):
        return remote(
            rows16.at[0, b, 3 + j], fleft.at[j], s_fright.at[j], r_fleft.at[j], right
        )

    def filt_left(j):
        return remote(
            rows16.at[0, b, j], fright.at[j], s_fleft.at[j], r_fright.at[j], left
        )

    def outer(s, carry):
        take_orbs(3 + s, 0)
        first_of([-2 - 2 * s, -1 - 2 * s, 12 + 2 * s, 13 + 2 * s])
        planes = [4 - 2 * s, 5 - 2 * s, 6 + 2 * s, 7 + 2 * s]
        xs, hs = hamiltonian(
            first, [p + 6 for p in planes], [pots[p + 6] for p in planes], w, ext
        )
        out = []
        for p, x, h in zip(planes, xs, hs):
            v = 0.25 * h - 2.0 * x - orbs[p + 12]
            second[p + 6] = v
            out.append(v)
        rows16[0, b, 2 - s] = jnp.concatenate(out[:2], axis=0).astype(BF)
        rows16[0, b, 3 + s] = jnp.concatenate(out[2:], axis=0).astype(BF)
        filt_left(2 - s).start()
        filt_right(s).start()
        around = edge & (s < AROUND)

        @pl.when(around)
        def _():
            to_mate(2 - s).start()
            to_mate(3 + s).start()

        @pl.when(jnp.logical_not(around))
        def _():
            to_z(0, 2 - s).start()
            to_z(0, 3 + s).start()

        to_c(0, 2 - s).start()
        to_c(0, 3 + s).start()
        return carry

    lax.fori_loop(0, 3, outer, 0)

    def pass_on(s, carry):
        come_z(0, 2 - s).wait_recv()
        forward(0, 2 - s).start()
        come_z(0, 3 + s).wait_recv()
        forward(0, 3 + s).start()
        return carry

    def local(g, carry):
        planes = [g * GROUP + j for j in range(GROUP)]
        _, hs = hamiltonian(
            second, [p + 6 for p in planes], [pots[p + 6] for p in planes], w, ext
        )
        for p, h in zip(planes, hs):
            applied[p] = h
        return carry

    lax.fori_loop(0, 3, local, 0)

    def add_halo(j):
        filt_right(j).wait_recv()
        filt_left(2 - j).wait_recv()
        from_left = fleft[j].astype(F32)
        from_right = fright[2 - j].astype(F32)
        near, far = 5 - 2 * j, 6 - 2 * j
        for p in range(7 - near):
            low = A[near + p] * from_left[8:]
            high = A[near + p] * from_right[:8]
            if p <= 6 - far:
                low = low + A[far + p] * from_left[:8]
                high = high + A[far + p] * from_right[8:]
            applied[p] += low
            applied[11 - p] += high

    @pl.when(jnp.logical_not(edge))
    def _():
        for q in ORDER[: 2 * AROUND]:
            to_mate(q).wait_recv()
            from_mate(q).start()

    add_halo(0)
    add_halo(1)
    pass_on(0, 0)
    pass_on(1, 0)
    add_halo(2)
    for q in ORDER:
        rows16[1, b, q] = jnp.concatenate([applied[2 * q], applied[2 * q + 1]], axis=0).astype(BF)
        to_z(1, q).start()
        to_c(1, q).start()
    pass_on(2, 0)

    pl.semaphore_wait(plane_in, 1)
    even[...] = jnp.zeros_like(even)
    odd[...] = jnp.zeros_like(odd)

    def come_on(q):
        come_z(1, q).wait_recv()
        forward(1, q).start()

    def gram(q, total):
        for a in range(2):
            come_c(a, q).wait_recv()
            come_f(a, q).wait_recv()
        load_sub(2 * q).wait()
        load_sub(2 * q + 1).wait()
        filt = jnp.concatenate([rows16[0, o, q] for o in range(4)], axis=0)
        appl = jnp.concatenate([rows16[1, o, q] for o in range(4)], axis=0)
        rows = jnp.concatenate([filt, appl], axis=0)
        nt = (((1,), (1,)), ((), ()))
        even[...] += lax.dot_general(sub[2 * q], rows, nt, preferred_element_type=F32)
        odd[...] += lax.dot_general(sub[2 * q + 1], rows, nt, preferred_element_type=F32)
        for c in range(16):
            v = filt[:, c * 128 : (c + 1) * 128].astype(F32)
            total = total + v * v
        return total

    def step(s, total):
        q = 2 - s // 2 + lax.rem(s, 2) * (2 * (s // 2) + 1)
        after = s + 1
        come_on(2 - after // 2 + lax.rem(after, 2) * (2 * (after // 2) + 1))
        return gram(q, total)

    come_on(2)
    squares = lax.fori_loop(0, 5, step, jnp.zeros((64, 128), F32))
    squares = gram(5, squares)

    from_even = even[...].T
    from_odd = odd[...].T
    for o in range(4):
        for a in range(2):
            at = a * 64 + o * 16
            block = from_even[at : at + 8] + from_odd[at + 8 : at + 16]
            for c in range(4):
                msg[pl.ds(o * 8, 8), a * 4 + c, :] = block[:, c * 128 : (c + 1) * 128]
        msg[pl.ds(o * 8, 8), 8, :] = squares[o * 16 : o * 16 + 8] + squares[o * 16 + 8 : o * 16 + 16]

    def to_all(k):
        t = lax.rem(d + k, DOM)
        return remote(msg.at[t], got.at[d], s_all.at[k], r_all.at[k], (t, b))

    def from_all(k):
        t = lax.rem(d + DOM - k, DOM)
        return remote(msg.at[t], got.at[t], s_all.at[k], r_all.at[k], (t, b))

    for k in range(1, DOM):
        to_all(k).start()
    got[d] = msg[d]

    def wait_sends(j, carry):
        orb_right(j).wait_send()
        orb_left(j).wait_send()
        for a in range(2):
            to_z(a, j).wait_send()
            to_c(a, j).wait_send()
            forward(a, j).wait_send()
        return carry

    lax.fori_loop(0, 6, wait_sends, 0)

    def wait_filt(j, carry):
        filt_right(j).wait_send()
        filt_left(j).wait_send()
        return carry

    lax.fori_loop(0, 3, wait_filt, 0)
    @pl.when(jnp.logical_not(edge))
    def _():
        for q in ORDER[: 2 * AROUND]:
            from_mate(q).wait_send()

    pot_right.wait_send()
    pot_left.wait_send()
    share(0).wait_send()
    share(1).wait_send()

    for k in range(1, DOM):
        to_all(k).wait_send()
    for k in range(1, DOM):
        from_all(k).wait_recv()
    total = got[0]
    for t in range(1, DOM):
        total = total + got[t]
    scale = jnp.sqrt(jnp.sum(total[8:], axis=1, keepdims=True) / CELLS + 1e-06)
    total = total[:8] / scale
    for c in range(4):
        both[0:1, c * 128 : (c + 1) * 128] = total[c : c + 1]
        both[1:2, c * 128 : (c + 1) * 128] = total[4 + c : 5 + c]


def shards(orbitals, potential, subspace):
    dma = pltpu.SemaphoreType.DMA
    both = pl.pallas_call(
        kernel,
        out_shape=jax.ShapeDtypeStruct((2, 512), F32),
        in_specs=[
            pl.BlockSpec(memory_space=pltpu.HBM),
            pl.BlockSpec(memory_space=pltpu.HBM),
            pl.BlockSpec(memory_space=pltpu.HBM),
        ],
        out_specs=pl.BlockSpec(memory_space=pltpu.VMEM),
        scratch_shapes=[
            pltpu.VMEM((12, PLANE), F32),
            pltpu.VMEM((36, 8, PLANE), F32),
            pltpu.VMEM((6, 16, PLANE), BF),
            pltpu.VMEM((6, 16, PLANE), BF),
            pltpu.VMEM((6, 16, PLANE), BF),
            pltpu.VMEM((24, 8, PLANE), F32),
            pltpu.VMEM((24, 8, PLANE), F32),
            pltpu.VMEM((12, 8, PLANE), F32),
            pltpu.VMEM((3, 16, PLANE), BF),
            pltpu.VMEM((3, 16, PLANE), BF),
            pltpu.VMEM((2, 4, 6, 16, PLANE), BF),
            pltpu.VMEM((6, 16, PLANE), BF),
            pltpu.VMEM((24, 1, PLANE), F32),
            pltpu.VMEM((GROUP, 2, 8, PLANE + 2 * EXT), F32),
            pltpu.VMEM((256, 256), BF),
            pltpu.VMEM((12, 512, PLANE), BF),
            pltpu.VMEM((512, 128), F32),
            pltpu.VMEM((512, 128), F32),
            pltpu.VMEM((DOM, 9, 128), F32),
            pltpu.VMEM((DOM, 9, 128), F32),
            pltpu.SemaphoreType.REGULAR, pltpu.SemaphoreType.REGULAR,
            dma(()), dma(()), dma((12,)),
            dma((6,)), dma((6,)), dma((6,)), dma((6,)), dma((2,)), dma((2,)), dma((2,)), dma((2,)),
            dma((3,)), dma((3,)), dma((3,)), dma((3,)),
            dma((12,)), dma((12,)), dma((12,)), dma((12,)), dma((12,)), dma((12,)),
            dma((6,)), dma((6,)), dma((DOM,)), dma((DOM,)),
        ],
        compiler_params=pltpu.CompilerParams(
            collective_id=0, has_side_effects=True, vmem_limit_bytes=64 * 2**20 - 10400 * 1024
        ),
    )(orbitals.transpose(1, 0, 2), potential, subspace.transpose(1, 0, 2))
    return both[0:1], both[1:2]


def solution(mesh):
    placed = (P("orb", "dom", None), P("dom", None), P("orb", "dom", None))
    return jax.shard_map(
        shards,
        mesh=mesh,
        in_specs=placed,
        out_specs=(P("dom", "orb"), P("dom", "orb")),
        check_vma=False,
    )
```

```python
import jax
import jax.numpy as jnp
from jax import lax
from jax.experimental import pallas as pl
from jax.experimental.pallas import tpu as pltpu
from jax.sharding import PartitionSpec as P

BF = jnp.bfloat16
F32 = jnp.float32
MESH = pl.DeviceIdType.MESH

coeffs = (
    -5369.0 / 1800.0,
    12.0 / 7.0,
    -15.0 / 56.0,
    10.0 / 189.0,
    -1.0 / 112.0,
    2.0 / 1925.0,
    -1.0 / 16632.0,
)
A = [-0.5 * c for c in coeffs]

NZ = 64
PLANE = 2048
EXT = 384
GROUP = 4
DOM = 32
AROUND = 1
ORDER = (2, 3, 1, 4, 0, 5)
CELLS = 786432


def z_matrix():
    row = lax.broadcasted_iota(jnp.int32, (128, 128), 0)
    col = lax.broadcasted_iota(jnp.int32, (128, 128), 1)
    same = (row >= NZ) == (col >= NZ)
    apart = (row - col) & (NZ - 1)
    m = jnp.zeros((128, 128), F32)
    for k in range(1, 7):
        m = jnp.where(same & ((apart == k) | (apart == NZ - k)), A[k], m)
    hi = m.astype(BF)
    lo = (m - hi.astype(F32)).astype(BF)
    top = jnp.concatenate([hi, lo], axis=1)
    low = jnp.concatenate([hi, jnp.zeros_like(hi)], axis=1)
    return jnp.concatenate([top, low], axis=0)


def hamiltonian(src, planes, pots, w, ext):
    xs = [src[i] for i in planes]
    lhs = []
    for x in xs:
        t = jnp.concatenate([x[:, c * 128 : (c + 1) * 128] for c in range(16)], axis=0)
        hi = t.astype(BF)
        lo = (t - hi.astype(F32)).astype(BF)
        lhs.append(jnp.concatenate([hi, lo], axis=1))
    z = jnp.dot(jnp.concatenate(lhs, axis=0), w[...], preferred_element_type=F32)
    z = z[:, :128] + z[:, 128:]
    outs = []
    for j, (i, x) in enumerate(zip(planes, xs)):
        turned = pltpu.roll(x, NZ, 1)
        for e, v in ((0, x), (1, turned)):
            ext[j, e, :, EXT : EXT + PLANE] = v
            ext[j, e, :, :EXT] = v[:, PLANE - EXT :]
            ext[j, e, :, EXT + PLANE :] = v[:, :EXT]

        def along_y(k):
            odd = k % 2
            start = EXT + NZ * (k + odd)
            return ext[j, odd, :, start : start + PLANE]

        acc = (3 * A[0] + pots[j]) * x
        acc = acc + jnp.concatenate(
            [z[j * 128 + c * 8 : j * 128 + c * 8 + 8] for c in range(16)], axis=1
        )
        for k in range(1, 7):
            acc = acc + A[k] * (
                (src[i + k] + src[i - k]) + (along_y(k) + along_y(-k))
            )
        outs.append(acc)
    return xs, outs


def kernel(
    orb_hbm, pot_hbm, sub_hbm, both,
    pot, orbs, own16, left16, right16, first, second, applied, fleft, fright, rows16, relay, pots, ext, w,
    sub, even, odd, msg, got,
    row_in, plane_in, s_pots, s_loc, s_sub, s_toright, s_toleft, r_left, r_right, s_pot, r_pot, s_share, r_share,
    s_fright, s_fleft, r_fleft, r_fright,
    s_z, r_z, s_c, r_c, s_f, r_f, s_relay, r_relay, s_all, r_all,
):
    d = lax.axis_index("dom")
    b = lax.axis_index("orb")
    right = (lax.rem(d + 1, DOM), b)
    left = (lax.rem(d + DOM - 1, DOM), b)
    b_z = lax.rem(b + 2, 4)
    b_c = b + 1 - 2 * lax.rem(b, 2)
    b_zc = lax.rem(b_c + 2, 4)
    x = lax.rem(d, 4)
    mate = d + 1 - 2 * lax.rem(x, 2)
    edge = (x == 0) | (x == 3)

    barrier = pltpu.get_barrier_semaphore()
    load = pltpu.make_async_copy(orb_hbm, orbs.at[pl.ds(12, 12)], s_loc)
    load.start()
    load_pot = pltpu.make_async_copy(pot_hbm, pot, s_pots)
    load_pot.start()

    beyond = d + 4 - 8 * lax.rem(d // 4, 2)
    same_y = [d - x + lax.rem(x + k, 4) for k in range(1, 4)]
    across_y = [lax.rem(d + 8 * k, DOM) for k in range(1, 4)]
    peers_in = [right, left, (d, b_z), (d, b_c), (d, b_zc), (mate, b_z)]
    peers_in += [(t, b) for t in [*same_y, *across_y, beyond]]
    for peer in peers_in:
        pl.semaphore_signal(barrier, inc=1, device_id=peer, device_id_type=MESH)

    def load_sub(p):
        return pltpu.make_async_copy(sub_hbm.at[p], sub.at[p], s_sub.at[p])

    def start_sub(p, carry):
        load_sub(p).start()
        return carry

    lax.fori_loop(0, 12, start_sub, 0)
    load_pot.wait()
    for p in range(12):
        pots[6 + p] = pot[p : p + 1, :]
    load.wait()

    def narrow(q, carry):
        own16[q] = jnp.concatenate([orbs[12 + 2 * q], orbs[13 + 2 * q]], axis=0).astype(BF)
        return carry

    lax.fori_loop(0, 6, narrow, 0)

    def remote(src, dst, ss, rs, device):
        return pltpu.make_async_remote_copy(
            src_ref=src, dst_ref=dst, send_sem=ss, recv_sem=rs,
            device_id=device, device_id_type=MESH,
        )

    def orb_right(q):
        return remote(own16.at[q], left16.at[q], s_toright.at[q], r_left.at[q], right)

    def orb_left(q):
        return remote(own16.at[q], right16.at[q], s_toleft.at[q], r_right.at[q], left)

    def half(start, o):
        at = pl.multiple_of(lax.rem(o, 2) * 1024, 1024)
        return pots.at[pl.ds(start, 6), :, pl.ds(at, 1024)]

    pot_right = remote(half(12, b), half(0, b), s_pot.at[0], r_pot.at[0], right)
    pot_left = remote(half(6, b), half(18, b), s_pot.at[1], r_pot.at[1], left)

    def share(side):
        mine = half(18 * side, b)
        return remote(mine, mine, s_share.at[side], r_share.at[side], (d, b_c))

    def shared(side):
        other = half(18 * side, b_c)
        return remote(other, other, s_share.at[side], r_share.at[side], (d, b_c))

    pl.semaphore_wait(barrier, len(peers_in))

    def send_orbs(j, carry):
        orb_right(5 - j).start()
        orb_left(j).start()
        return carry

    pot_right.start()
    pot_left.start()
    lax.fori_loop(0, 6, send_orbs, 0)

    for t in across_y:
        pl.semaphore_signal(row_in, inc=1, device_id=(t, b), device_id_type=MESH)

    def widen(src, q, dst, at):
        both = src[q].astype(F32)
        dst[at] = both[:8]
        dst[at + 1] = both[8:]

    def take_orbs(j, carry):
        orb_right(5 - j).wait_recv()
        widen(left16, 5 - j, orbs, 2 * (5 - j))
        orb_left(j).wait_recv()
        widen(right16, j, orbs, 24 + 2 * j)
        return carry

    w[...] = z_matrix()
    second[pl.ds(0, 6)] = jnp.zeros((6, 8, PLANE), F32)
    second[pl.ds(18, 6)] = jnp.zeros((6, 8, PLANE), F32)
    pot_right.wait_recv()
    share(0).start()
    pot_left.wait_recv()
    share(1).start()
    lax.fori_loop(0, 3, take_orbs, 0)

    def first_of(planes):
        xs, hs = hamiltonian(
            orbs, [p + 12 for p in planes], [pots[p + 6] for p in planes], w, ext
        )
        for p, x, h in zip(planes, xs, hs):
            first[p + 6] = 0.125 * h - x

    def inner(g, carry):
        first_of([g * GROUP + j for j in range(GROUP)])
        return carry

    lax.fori_loop(0, 3, inner, 0)
    shared(0).wait_recv()
    shared(1).wait_recv()
    pl.semaphore_wait(row_in, len(across_y))
    pl.semaphore_signal(plane_in, inc=1, device_id=(beyond, b), device_id_type=MESH)

    def to_z(a, q):
        n = a * 6 + q
        return remote(
            rows16.at[a, b, q], rows16.at[a, b, q], s_z.at[n], r_z.at[n], (d, b_z)
        )

    def to_c(a, q):
        n = a * 6 + q
        return remote(
            rows16.at[a, b, q], rows16.at[a, b, q], s_c.at[n], r_c.at[n], (d, b_c)
        )

    def forward(a, q):
        n = a * 6 + q
        return remote(
            rows16.at[a, b_z, q], rows16.at[a, b_z, q], s_f.at[n], r_f.at[n], (d, b_c)
        )

    def come_z(a, q):
        n = a * 6 + q
        return remote(
            rows16.at[a, b_z, q], rows16.at[a, b_z, q], s_z.at[n], r_z.at[n], (d, b_z)
        )

    def come_c(a, q):
        n = a * 6 + q
        return remote(
            rows16.at[a, b_c, q], rows16.at[a, b_c, q], s_c.at[n], r_c.at[n], (d, b_c)
        )

    def come_f(a, q):
        n = a * 6 + q
        return remote(
            rows16.at[a, b_zc, q], rows16.at[a, b_zc, q], s_f.at[n], r_f.at[n], (d, b_c)
        )

    def to_mate(q):
        return remote(
            rows16.at[0, b, q], relay.at[q], s_z.at[q], r_relay.at[q], (mate, b_z)
        )

    def from_mate(q):
        return remote(
            relay.at[q], rows16.at[0, b_z, q], s_relay.at[q], r_z.at[q], (mate, b)
        )

    def filt_right(j):
        return remote(
            rows16.at[0, b, 3 + j], fleft.at[j], s_fright.at[j], r_fleft.at[j], right
        )

    def filt_left(j):
        return remote(
            rows16.at[0, b, j], fright.at[j], s_fleft.at[j], r_fright.at[j], left
        )

    def outer(s, carry):
        take_orbs(3 + s, 0)
        first_of([-2 - 2 * s, -1 - 2 * s, 12 + 2 * s, 13 + 2 * s])
        planes = [4 - 2 * s, 5 - 2 * s, 6 + 2 * s, 7 + 2 * s]
        xs, hs = hamiltonian(
            first, [p + 6 for p in planes], [pots[p + 6] for p in planes], w, ext
        )
        out = []
        for p, x, h in zip(planes, xs, hs):
            v = 0.25 * h - 2.0 * x - orbs[p + 12]
            second[p + 6] = v
            out.append(v)
        rows16[0, b, 2 - s] = jnp.concatenate(out[:2], axis=0).astype(BF)
        rows16[0, b, 3 + s] = jnp.concatenate(out[2:], axis=0).astype(BF)
        filt_left(2 - s).start()
        filt_right(s).start()
        around = edge & (s < AROUND)

        @pl.when(around)
        def _():
            to_mate(2 - s).start()
            to_z(0, 3 + s).start()

        @pl.when(jnp.logical_not(around))
        def _():
            to_z(0, 2 - s).start()
            to_z(0, 3 + s).start()

        to_c(0, 2 - s).start()
        to_c(0, 3 + s).start()
        return carry

    lax.fori_loop(0, 3, outer, 0)

    def pass_on(s, carry):
        come_z(0, 2 - s).wait_recv()
        forward(0, 2 - s).start()
        come_z(0, 3 + s).wait_recv()
        forward(0, 3 + s).start()
        return carry

    def local(g, carry):
        planes = [g * GROUP + j for j in range(GROUP)]
        _, hs = hamiltonian(
            second, [p + 6 for p in planes], [pots[p + 6] for p in planes], w, ext
        )
        for p, h in zip(planes, hs):
            applied[p] = h
        return carry

    lax.fori_loop(0, 3, local, 0)

    def add_halo(j):
        filt_right(j).wait_recv()
        filt_left(2 - j).wait_recv()
        from_left = fleft[j].astype(F32)
        from_right = fright[2 - j].astype(F32)
        near, far = 5 - 2 * j, 6 - 2 * j
        for p in reversed(range(7 - near)):
            low = A[near + p] * from_left[8:]
            high = A[near + p] * from_right[:8]
            if p <= 6 - far:
                low = low + A[far + p] * from_left[:8]
                high = high + A[far + p] * from_right[8:]
            applied[p] += low
            applied[11 - p] += high

    @pl.when(jnp.logical_not(edge))
    def _():
        for q in ORDER[:AROUND]:
            to_mate(q).wait_recv()
            from_mate(q).start()

    add_halo(0)
    add_halo(1)
    pass_on(0, 0)
    pass_on(1, 0)
    add_halo(2)
    for q in ORDER:
        rows16[1, b, q] = jnp.concatenate([applied[2 * q], applied[2 * q + 1]], axis=0).astype(BF)
        to_z(1, q).start()
        to_c(1, q).start()
    pass_on(2, 0)

    pl.semaphore_wait(plane_in, 1)
    even[...] = jnp.zeros_like(even)
    odd[...] = jnp.zeros_like(odd)

    def come_on(q):
        come_z(1, q).wait_recv()
        forward(1, q).start()

    def gram(q, total):
        for a in range(2):
            come_c(a, q).wait_recv()
            come_f(a, q).wait_recv()
        load_sub(2 * q).wait()
        load_sub(2 * q + 1).wait()
        filt = jnp.concatenate([rows16[0, o, q] for o in range(4)], axis=0)
        appl = jnp.concatenate([rows16[1, o, q] for o in range(4)], axis=0)
        rows = jnp.concatenate([filt, appl], axis=0)
        nt = (((1,), (1,)), ((), ()))
        even[...] += lax.dot_general(sub[2 * q], rows, nt, preferred_element_type=F32)
        odd[...] += lax.dot_general(sub[2 * q + 1], rows, nt, preferred_element_type=F32)
        for c in range(16):
            v = filt[:, c * 128 : (c + 1) * 128].astype(F32)
            total = total + v * v
        return total

    def step(s, total):
        q = 2 - s // 2 + lax.rem(s, 2) * (2 * (s // 2) + 1)
        after = s + 1
        come_on(2 - after // 2 + lax.rem(after, 2) * (2 * (after // 2) + 1))
        return gram(q, total)

    come_on(2)
    squares = lax.fori_loop(0, 5, step, jnp.zeros((64, 128), F32))
    squares = gram(5, squares)

    by_row = (even[...] + pltpu.roll(odd[...], 120, 1)).T
    for o in range(4):
        for a in range(2):
            at = a * 64 + o * 16
            block = by_row[at : at + 8]
            for c in range(4):
                msg[pl.ds(o * 8, 8), a * 4 + c, :] = block[:, c * 128 : (c + 1) * 128]
        msg[pl.ds(o * 8, 8), 8, :] = squares[o * 16 : o * 16 + 8] + squares[o * 16 + 8 : o * 16 + 16]

    def to_all(k):
        t = lax.rem(d + k, DOM)
        return remote(msg.at[t], got.at[d], s_all.at[k], r_all.at[k], (t, b))

    def from_all(k):
        t = lax.rem(d + DOM - k, DOM)
        return remote(msg.at[t], got.at[t], s_all.at[k], r_all.at[k], (t, b))

    for k in range(1, DOM):
        to_all(k).start()
    got[d] = msg[d]

    def wait_sends(j, carry):
        orb_right(j).wait_send()
        orb_left(j).wait_send()
        for a in range(2):
            to_z(a, j).wait_send()
            to_c(a, j).wait_send()
            forward(a, j).wait_send()
        return carry

    lax.fori_loop(0, 6, wait_sends, 0)

    def wait_filt(j, carry):
        filt_right(j).wait_send()
        filt_left(j).wait_send()
        return carry

    lax.fori_loop(0, 3, wait_filt, 0)
    @pl.when(jnp.logical_not(edge))
    def _():
        for q in ORDER[:AROUND]:
            from_mate(q).wait_send()

    pot_right.wait_send()
    pot_left.wait_send()
    share(0).wait_send()
    share(1).wait_send()

    for k in range(1, DOM):
        to_all(k).wait_send()
    for k in range(1, DOM):
        from_all(k).wait_recv()
    total = got[0]
    for t in range(1, DOM):
        total = total + got[t]
    scale = jnp.sqrt(jnp.sum(total[8:], axis=1, keepdims=True) / CELLS + 1e-06)
    total = total[:8] / scale
    for c in range(4):
        both[0:1, c * 128 : (c + 1) * 128] = total[c : c + 1]
        both[1:2, c * 128 : (c + 1) * 128] = total[4 + c : 5 + c]


def shards(orbitals, potential, subspace):
    dma = pltpu.SemaphoreType.DMA
    both = pl.pallas_call(
        kernel,
        out_shape=jax.ShapeDtypeStruct((2, 512), F32),
        in_specs=[
            pl.BlockSpec(memory_space=pltpu.HBM),
            pl.BlockSpec(memory_space=pltpu.HBM),
            pl.BlockSpec(memory_space=pltpu.HBM),
        ],
        out_specs=pl.BlockSpec(memory_space=pltpu.VMEM),
        scratch_shapes=[
            pltpu.VMEM((12, PLANE), F32),
            pltpu.VMEM((36, 8, PLANE), F32),
            pltpu.VMEM((6, 16, PLANE), BF),
            pltpu.VMEM((6, 16, PLANE), BF),
            pltpu.VMEM((6, 16, PLANE), BF),
            pltpu.VMEM((24, 8, PLANE), F32),
            pltpu.VMEM((24, 8, PLANE), F32),
            pltpu.VMEM((12, 8, PLANE), F32),
            pltpu.VMEM((3, 16, PLANE), BF),
            pltpu.VMEM((3, 16, PLANE), BF),
            pltpu.VMEM((2, 4, 6, 16, PLANE), BF),
            pltpu.VMEM((6, 16, PLANE), BF),
            pltpu.VMEM((24, 1, PLANE), F32),
            pltpu.VMEM((GROUP, 2, 8, PLANE + 2 * EXT), F32),
            pltpu.VMEM((256, 256), BF),
            pltpu.VMEM((12, 512, PLANE), BF),
            pltpu.VMEM((512, 128), F32),
            pltpu.VMEM((512, 128), F32),
            pltpu.VMEM((DOM, 9, 128), F32),
            pltpu.VMEM((DOM, 9, 128), F32),
            pltpu.SemaphoreType.REGULAR, pltpu.SemaphoreType.REGULAR,
            dma(()), dma(()), dma((12,)),
            dma((6,)), dma((6,)), dma((6,)), dma((6,)), dma((2,)), dma((2,)), dma((2,)), dma((2,)),
            dma((3,)), dma((3,)), dma((3,)), dma((3,)),
            dma((12,)), dma((12,)), dma((12,)), dma((12,)), dma((12,)), dma((12,)),
            dma((6,)), dma((6,)), dma((DOM,)), dma((DOM,)),
        ],
        compiler_params=pltpu.CompilerParams(
            collective_id=0, has_side_effects=True, vmem_limit_bytes=64 * 2**20 - 10400 * 1024
        ),
    )(orbitals.transpose(1, 0, 2), potential, subspace.transpose(1, 0, 2))
    return both[0:1], both[1:2]


def solution(mesh):
    placed = (P("orb", "dom", None), P("dom", None), P("orb", "dom", None))
    return jax.shard_map(
        shards,
        mesh=mesh,
        in_specs=placed,
        out_specs=(P("dom", "orb"), P("dom", "orb")),
        check_vma=False,
    )
```

```python
import jax
import jax.numpy as jnp
from jax import lax
from jax.experimental import pallas as pl
from jax.experimental.pallas import tpu as pltpu
from jax.sharding import PartitionSpec as P

BF = jnp.bfloat16
F32 = jnp.float32
MESH = pl.DeviceIdType.MESH

coeffs = (
    -5369.0 / 1800.0,
    12.0 / 7.0,
    -15.0 / 56.0,
    10.0 / 189.0,
    -1.0 / 112.0,
    2.0 / 1925.0,
    -1.0 / 16632.0,
)
A = [-0.5 * c for c in coeffs]

NZ = 64
PLANE = 2048
EXT = 384
GROUP = 4
DOM = 32
AROUND = 1
ORDER = (2, 3, 1, 4, 0, 5)
CELLS = 786432


def z_matrix():
    row = lax.broadcasted_iota(jnp.int32, (128, 128), 0)
    col = lax.broadcasted_iota(jnp.int32, (128, 128), 1)
    same = (row >= NZ) == (col >= NZ)
    apart = (row - col) & (NZ - 1)
    m = jnp.zeros((128, 128), F32)
    for k in range(1, 7):
        m = jnp.where(same & ((apart == k) | (apart == NZ - k)), A[k], m)
    hi = m.astype(BF)
    lo = (m - hi.astype(F32)).astype(BF)
    top = jnp.concatenate([hi, lo], axis=1)
    low = jnp.concatenate([hi, jnp.zeros_like(hi)], axis=1)
    return jnp.concatenate([top, low], axis=0)


def hamiltonian(src, planes, pots, w, ext):
    xs = [src[i] for i in planes]
    lhs = []
    for x in xs:
        t = jnp.concatenate([x[:, c * 128 : (c + 1) * 128] for c in range(16)], axis=0)
        hi = t.astype(BF)
        lo = (t - hi.astype(F32)).astype(BF)
        lhs.append(jnp.concatenate([hi, lo], axis=1))
    z = jnp.dot(jnp.concatenate(lhs, axis=0), w[...], preferred_element_type=F32)
    z = z[:, :128] + z[:, 128:]
    outs = []
    for j, (i, x) in enumerate(zip(planes, xs)):
        turned = pltpu.roll(x, NZ, 1)
        for e, v in ((0, x), (1, turned)):
            ext[j, e, :, EXT : EXT + PLANE] = v
            ext[j, e, :, :EXT] = v[:, PLANE - EXT :]
            ext[j, e, :, EXT + PLANE :] = v[:, :EXT]

        def along_y(k):
            odd = k % 2
            start = EXT + NZ * (k + odd)
            return ext[j, odd, :, start : start + PLANE]

        acc = (3 * A[0] + pots[j]) * x
        acc = acc + jnp.concatenate(
            [z[j * 128 + c * 8 : j * 128 + c * 8 + 8] for c in range(16)], axis=1
        )
        for k in range(1, 7):
            acc = acc + A[k] * (
                (src[i + k] + src[i - k]) + (along_y(k) + along_y(-k))
            )
        outs.append(acc)
    return xs, outs


def kernel(
    orb_hbm, pot_hbm, sub_hbm, both,
    pot, orbs, own16, left16, right16, first, second, applied, fleft, fright, rows16, relay, pots, ext, w,
    sub, even, odd, msg, got,
    row_in, plane_in, s_pots, s_loc, s_sub, s_toright, s_toleft, r_left, r_right, s_pot, r_pot, s_share, r_share,
    s_fright, s_fleft, r_fleft, r_fright,
    s_z, r_z, s_c, r_c, s_f, r_f, s_relay, r_relay, s_all, r_all,
):
    d = lax.axis_index("dom")
    b = lax.axis_index("orb")
    right = (lax.rem(d + 1, DOM), b)
    left = (lax.rem(d + DOM - 1, DOM), b)
    b_z = lax.rem(b + 2, 4)
    b_c = b + 1 - 2 * lax.rem(b, 2)
    b_zc = lax.rem(b_c + 2, 4)
    x = lax.rem(d, 4)
    mate = d + 1 - 2 * lax.rem(x, 2)
    edge = (x == 0) | (x == 3)

    barrier = pltpu.get_barrier_semaphore()
    load = pltpu.make_async_copy(orb_hbm, orbs.at[pl.ds(12, 12)], s_loc)
    load.start()
    load_pot = pltpu.make_async_copy(pot_hbm, pot, s_pots)
    load_pot.start()

    beyond = d + 4 - 8 * lax.rem(d // 4, 2)
    same_y = [d - x + lax.rem(x + k, 4) for k in range(1, 4)]
    across_y = [lax.rem(d + 8 * k, DOM) for k in range(1, 4)]
    peers_in = [right, left, (d, b_z), (d, b_c), (d, b_zc), (mate, b_z)]
    peers_in += [(t, b) for t in [*same_y, *across_y, beyond]]
    for peer in peers_in:
        pl.semaphore_signal(barrier, inc=1, device_id=peer, device_id_type=MESH)

    def load_sub(p):
        return pltpu.make_async_copy(sub_hbm.at[p], sub.at[p], s_sub.at[p])

    def start_sub(p, carry):
        load_sub(p).start()
        return carry

    load_pot.wait()
    for p in range(12):
        pots[6 + p] = pot[p : p + 1, :]
    load.wait()

    def narrow(q, carry):
        own16[q] = jnp.concatenate([orbs[12 + 2 * q], orbs[13 + 2 * q]], axis=0).astype(BF)
        return carry

    lax.fori_loop(0, 6, narrow, 0)

    def remote(src, dst, ss, rs, device):
        return pltpu.make_async_remote_copy(
            src_ref=src, dst_ref=dst, send_sem=ss, recv_sem=rs,
            device_id=device, device_id_type=MESH,
        )

    def orb_right(q):
        return remote(own16.at[q], left16.at[q], s_toright.at[q], r_left.at[q], right)

    def orb_left(q):
        return remote(own16.at[q], right16.at[q], s_toleft.at[q], r_right.at[q], left)

    def half(start, o):
        at = pl.multiple_of(lax.rem(o, 2) * 1024, 1024)
        return pots.at[pl.ds(start, 6), :, pl.ds(at, 1024)]

    pot_right = remote(half(12, b), half(0, b), s_pot.at[0], r_pot.at[0], right)
    pot_left = remote(half(6, b), half(18, b), s_pot.at[1], r_pot.at[1], left)

    def share(side):
        mine = half(18 * side, b)
        return remote(mine, mine, s_share.at[side], r_share.at[side], (d, b_c))

    def shared(side):
        other = half(18 * side, b_c)
        return remote(other, other, s_share.at[side], r_share.at[side], (d, b_c))

    pl.semaphore_wait(barrier, len(peers_in))

    def send_orbs(j, carry):
        orb_right(5 - j).start()
        orb_left(j).start()
        return carry

    pot_right.start()
    pot_left.start()
    lax.fori_loop(0, 6, send_orbs, 0)

    for t in across_y:
        pl.semaphore_signal(row_in, inc=1, device_id=(t, b), device_id_type=MESH)

    def widen(src, q, dst, at):
        both = src[q].astype(F32)
        dst[at] = both[:8]
        dst[at + 1] = both[8:]

    def take_orbs(j, carry):
        orb_right(5 - j).wait_recv()
        widen(left16, 5 - j, orbs, 2 * (5 - j))
        orb_left(j).wait_recv()
        widen(right16, j, orbs, 24 + 2 * j)
        return carry

    lax.fori_loop(0, 12, start_sub, 0)
    w[...] = z_matrix()
    second[pl.ds(0, 6)] = jnp.zeros((6, 8, PLANE), F32)
    second[pl.ds(18, 6)] = jnp.zeros((6, 8, PLANE), F32)
    pot_right.wait_recv()
    share(0).start()
    pot_left.wait_recv()
    share(1).start()
    lax.fori_loop(0, 3, take_orbs, 0)

    def first_of(planes):
        xs, hs = hamiltonian(
            orbs, [p + 12 for p in planes], [pots[p + 6] for p in planes], w, ext
        )
        for p, x, h in zip(planes, xs, hs):
            first[p + 6] = 0.125 * h - x

    def inner(g, carry):
        first_of([g * GROUP + j for j in range(GROUP)])
        return carry

    lax.fori_loop(0, 3, inner, 0)
    shared(0).wait_recv()
    shared(1).wait_recv()
    pl.semaphore_wait(row_in, len(across_y))
    pl.semaphore_signal(plane_in, inc=1, device_id=(beyond, b), device_id_type=MESH)

    def to_z(a, q):
        n = a * 6 + q
        return remote(
            rows16.at[a, b, q], rows16.at[a, b, q], s_z.at[n], r_z.at[n], (d, b_z)
        )

    def to_c(a, q):
        n = a * 6 + q
        return remote(
            rows16.at[a, b, q], rows16.at[a, b, q], s_c.at[n], r_c.at[n], (d, b_c)
        )

    def forward(a, q):
        n = a * 6 + q
        return remote(
            rows16.at[a, b_z, q], rows16.at[a, b_z, q], s_f.at[n], r_f.at[n], (d, b_c)
        )

    def come_z(a, q):
        n = a * 6 + q
        return remote(
            rows16.at[a, b_z, q], rows16.at[a, b_z, q], s_z.at[n], r_z.at[n], (d, b_z)
        )

    def come_c(a, q):
        n = a * 6 + q
        return remote(
            rows16.at[a, b_c, q], rows16.at[a, b_c, q], s_c.at[n], r_c.at[n], (d, b_c)
        )

    def come_f(a, q):
        n = a * 6 + q
        return remote(
            rows16.at[a, b_zc, q], rows16.at[a, b_zc, q], s_f.at[n], r_f.at[n], (d, b_c)
        )

    def to_mate(q):
        return remote(
            rows16.at[0, b, q], relay.at[q], s_z.at[q], r_relay.at[q], (mate, b_z)
        )

    def from_mate(q):
        return remote(
            relay.at[q], rows16.at[0, b_z, q], s_relay.at[q], r_z.at[q], (mate, b)
        )

    def filt_right(j):
        return remote(
            rows16.at[0, b, 3 + j], fleft.at[j], s_fright.at[j], r_fleft.at[j], right
        )

    def filt_left(j):
        return remote(
            rows16.at[0, b, j], fright.at[j], s_fleft.at[j], r_fright.at[j], left
        )

    def outer(s, carry):
        take_orbs(3 + s, 0)
        first_of([-2 - 2 * s, -1 - 2 * s, 12 + 2 * s, 13 + 2 * s])
        planes = [4 - 2 * s, 5 - 2 * s, 6 + 2 * s, 7 + 2 * s]
        xs, hs = hamiltonian(
            first, [p + 6 for p in planes], [pots[p + 6] for p in planes], w, ext
        )
        out = []
        for p, x, h in zip(planes, xs, hs):
            v = 0.25 * h - 2.0 * x - orbs[p + 12]
            second[p + 6] = v
            out.append(v)
        rows16[0, b, 2 - s] = jnp.concatenate(out[:2], axis=0).astype(BF)
        rows16[0, b, 3 + s] = jnp.concatenate(out[2:], axis=0).astype(BF)
        filt_left(2 - s).start()
        filt_right(s).start()
        around = edge & (s < AROUND)

        @pl.when(around)
        def _():
            to_mate(2 - s).start()
            to_z(0, 3 + s).start()

        @pl.when(jnp.logical_not(around))
        def _():
            to_z(0, 2 - s).start()
            to_z(0, 3 + s).start()

        to_c(0, 2 - s).start()
        to_c(0, 3 + s).start()
        return carry

    lax.fori_loop(0, 3, outer, 0)

    def pass_on(s, carry):
        come_z(0, 2 - s).wait_recv()
        forward(0, 2 - s).start()
        come_z(0, 3 + s).wait_recv()
        forward(0, 3 + s).start()
        return carry

    def local(g, carry):
        planes = [g * GROUP + j for j in range(GROUP)]
        _, hs = hamiltonian(
            second, [p + 6 for p in planes], [pots[p + 6] for p in planes], w, ext
        )
        for p, h in zip(planes, hs):
            applied[p] = h
        return carry

    lax.fori_loop(0, 3, local, 0)

    def add_halo(j):
        filt_right(j).wait_recv()
        filt_left(2 - j).wait_recv()
        from_left = fleft[j].astype(F32)
        from_right = fright[2 - j].astype(F32)
        near, far = 5 - 2 * j, 6 - 2 * j
        for p in reversed(range(7 - near)):
            low = A[near + p] * from_left[8:]
            high = A[near + p] * from_right[:8]
            if p <= 6 - far:
                low = low + A[far + p] * from_left[:8]
                high = high + A[far + p] * from_right[8:]
            applied[p] += low
            applied[11 - p] += high

    @pl.when(jnp.logical_not(edge))
    def _():
        for q in ORDER[:AROUND]:
            to_mate(q).wait_recv()
            from_mate(q).start()

    add_halo(0)
    add_halo(1)
    pass_on(0, 0)
    pass_on(1, 0)
    add_halo(2)
    for q in ORDER:
        rows16[1, b, q] = jnp.concatenate([applied[2 * q], applied[2 * q + 1]], axis=0).astype(BF)
        to_z(1, q).start()
        to_c(1, q).start()
    pass_on(2, 0)

    pl.semaphore_wait(plane_in, 1)
    even[...] = jnp.zeros_like(even)
    odd[...] = jnp.zeros_like(odd)

    def come_on(q):
        come_z(1, q).wait_recv()
        forward(1, q).start()

    def gram(q, total):
        for a in range(2):
            come_c(a, q).wait_recv()
            come_f(a, q).wait_recv()
        load_sub(2 * q).wait()
        load_sub(2 * q + 1).wait()
        filt = jnp.concatenate([rows16[0, o, q] for o in range(4)], axis=0)
        appl = jnp.concatenate([rows16[1, o, q] for o in range(4)], axis=0)
        rows = jnp.concatenate([filt, appl], axis=0)
        nt = (((1,), (1,)), ((), ()))
        even[...] += lax.dot_general(sub[2 * q], rows, nt, preferred_element_type=F32)
        odd[...] += lax.dot_general(sub[2 * q + 1], rows, nt, preferred_element_type=F32)
        for c in range(16):
            v = filt[:, c * 128 : (c + 1) * 128].astype(F32)
            total = total + v * v
        return total

    def step(s, total):
        q = 2 - s // 2 + lax.rem(s, 2) * (2 * (s // 2) + 1)
        after = s + 1
        come_on(2 - after // 2 + lax.rem(after, 2) * (2 * (after // 2) + 1))
        return gram(q, total)

    come_on(2)
    squares = lax.fori_loop(0, 5, step, jnp.zeros((64, 128), F32))
    squares = gram(5, squares)

    by_row = (even[...] + pltpu.roll(odd[...], 120, 1)).T
    for o in range(4):
        for a in range(2):
            at = a * 64 + o * 16
            block = by_row[at : at + 8]
            for c in range(4):
                msg[pl.ds(o * 8, 8), a * 4 + c, :] = block[:, c * 128 : (c + 1) * 128]
        msg[pl.ds(o * 8, 8), 8, :] = squares[o * 16 : o * 16 + 8] + squares[o * 16 + 8 : o * 16 + 16]

    def to_all(k):
        t = lax.rem(d + k, DOM)
        return remote(msg.at[t], got.at[d], s_all.at[k], r_all.at[k], (t, b))

    def from_all(k):
        t = lax.rem(d + DOM - k, DOM)
        return remote(msg.at[t], got.at[t], s_all.at[k], r_all.at[k], (t, b))

    for k in range(1, DOM):
        to_all(k).start()
    got[d] = msg[d]

    def wait_sends(j, carry):
        orb_right(j).wait_send()
        orb_left(j).wait_send()
        for a in range(2):
            to_z(a, j).wait_send()
            to_c(a, j).wait_send()
            forward(a, j).wait_send()
        return carry

    lax.fori_loop(0, 6, wait_sends, 0)

    def wait_filt(j, carry):
        filt_right(j).wait_send()
        filt_left(j).wait_send()
        return carry

    lax.fori_loop(0, 3, wait_filt, 0)
    @pl.when(jnp.logical_not(edge))
    def _():
        for q in ORDER[:AROUND]:
            from_mate(q).wait_send()

    pot_right.wait_send()
    pot_left.wait_send()
    share(0).wait_send()
    share(1).wait_send()

    for k in range(1, DOM):
        to_all(k).wait_send()
    for k in range(1, DOM):
        from_all(k).wait_recv()
    total = got[0]
    for t in range(1, DOM):
        total = total + got[t]
    scale = jnp.sqrt(jnp.sum(total[8:], axis=1, keepdims=True) / CELLS + 1e-06)
    total = total[:8] / scale
    for c in range(4):
        both[0:1, c * 128 : (c + 1) * 128] = total[c : c + 1]
        both[1:2, c * 128 : (c + 1) * 128] = total[4 + c : 5 + c]


def shards(orbitals, potential, subspace):
    dma = pltpu.SemaphoreType.DMA
    both = pl.pallas_call(
        kernel,
        out_shape=jax.ShapeDtypeStruct((2, 512), F32),
        in_specs=[
            pl.BlockSpec(memory_space=pltpu.HBM),
            pl.BlockSpec(memory_space=pltpu.HBM),
            pl.BlockSpec(memory_space=pltpu.HBM),
        ],
        out_specs=pl.BlockSpec(memory_space=pltpu.VMEM),
        scratch_shapes=[
            pltpu.VMEM((12, PLANE), F32),
            pltpu.VMEM((36, 8, PLANE), F32),
            pltpu.VMEM((6, 16, PLANE), BF),
            pltpu.VMEM((6, 16, PLANE), BF),
            pltpu.VMEM((6, 16, PLANE), BF),
            pltpu.VMEM((24, 8, PLANE), F32),
            pltpu.VMEM((24, 8, PLANE), F32),
            pltpu.VMEM((12, 8, PLANE), F32),
            pltpu.VMEM((3, 16, PLANE), BF),
            pltpu.VMEM((3, 16, PLANE), BF),
            pltpu.VMEM((2, 4, 6, 16, PLANE), BF),
            pltpu.VMEM((6, 16, PLANE), BF),
            pltpu.VMEM((24, 1, PLANE), F32),
            pltpu.VMEM((GROUP, 2, 8, PLANE + 2 * EXT), F32),
            pltpu.VMEM((256, 256), BF),
            pltpu.VMEM((12, 512, PLANE), BF),
            pltpu.VMEM((512, 128), F32),
            pltpu.VMEM((512, 128), F32),
            pltpu.VMEM((DOM, 9, 128), F32),
            pltpu.VMEM((DOM, 9, 128), F32),
            pltpu.SemaphoreType.REGULAR, pltpu.SemaphoreType.REGULAR,
            dma(()), dma(()), dma((12,)),
            dma((6,)), dma((6,)), dma((6,)), dma((6,)), dma((2,)), dma((2,)), dma((2,)), dma((2,)),
            dma((3,)), dma((3,)), dma((3,)), dma((3,)),
            dma((12,)), dma((12,)), dma((12,)), dma((12,)), dma((12,)), dma((12,)),
            dma((6,)), dma((6,)), dma((DOM,)), dma((DOM,)),
        ],
        compiler_params=pltpu.CompilerParams(
            collective_id=0, has_side_effects=True, vmem_limit_bytes=64 * 2**20 - 10400 * 1024
        ),
    )(orbitals.transpose(1, 0, 2), potential, subspace.transpose(1, 0, 2))
    return both[0:1], both[1:2]


def solution(mesh):
    placed = (P("orb", "dom", None), P("dom", None), P("orb", "dom", None))
    return jax.shard_map(
        shards,
        mesh=mesh,
        in_specs=placed,
        out_specs=(P("dom", "orb"), P("dom", "orb")),
        check_vma=False,
    )
```
